32 devices in a mesh: tm: 4 (over x, core), expert: 8 (over z, y).
Axes of the slice: x: 2, y: 2, z: 4, core: 2. Of those that a mesh axis runs over, the one named last changes fastest.
Arguments:
- tokens: bfloat16 [8, 32, 64, 1280], P('expert', 'tm'), may hold values from -6 to 6
- time_taps: float32 [3, 1280], replicated, may hold values from -3 to 3
- norm_gain: float32 [1280], replicated, may hold values from 0.5 to 1.5
- expert_ids: int32 [8, 2048, 2], P('expert'), may hold values from 0 to 7, as said below
- priority_ranks: int32 [8, 2048, 2], P('expert'), may hold values from 0 to 256, as said below
- keep_mask: int32 [8, 2048, 2], P('expert'), may hold values from 0 to 1, as said below
- gate_weights: float32 [8, 2048, 2], P('expert'), may hold values from 0.2 to 1
- up_weight: bfloat16 [8, 1280, 5120], P('expert', None, 'tm'), may hold values from -0.15625 to 0.15625
- down_weight: bfloat16 [8, 5120, 1280], P('expert', 'tm'), may hold values from -0.078125 to 0.078125
- attn_gain: float32 [1280], replicated, may hold values from 0.5 to 1.5
- qkv_weight: bfloat16 [3, 1280, 1280], P(None, None, 'tm'), may hold values from -0.15625 to 0.15625
Outputs:
- stream: bfloat16 [8, 32, 64, 1280], P('expert', 'tm')
- qkv_rows: bfloat16 [3, 8, 2048, 1280], P(None, 'expert', None, 'tm')
The draws below stay inside these ranges and needn't reach their ends.
Inputs may be any that keep to these rules, and one draw needn't show every extreme that they name: `expert_ids`: the two experts of a token differ. priority_ranks[b, t, k] counts the assignments of clip b to the same expert that come earlier in batch-priority order, and is given as 256 where that count is 256 or more; every first choice of a clip comes before every second choice. Within a clip the kept assignments of one expert have distinct ranks. keep_mask is 1 exactly where priority_ranks < 256, so every expert receives at most 256 rows from each clip, and exactly 256 for some expert of every clip.
All inputs are finite; a program needn't handle non-finite values.
Results may differ from the reference program's by a relative error of at most 0.008.
Values may be sent and summed in bfloat16 or wider, within the bound.
No kernel may reach another device: no remote copies, remote signals or barrier semaphores. Data moves between devices by JAX's collectives and lax.ppermute only.
A program may use at most 128 MiB of HBM per device.

```python
import jax
import jax.numpy as jnp
from jax import lax

D = 1280
FF = 5120
TOPK = 2
FRAMES = 32
PATCHES = 64
EXPERTS = 8
CLIPS = 8
ROWS = 2048
CAP = 256
FF_DEV = 1280
N_TM = 4


def route_tables(key):
    key_list = jax.random.split(key, 5)
    draw_base = jax.random.randint(key_list[0], (CLIPS, ROWS), 0, EXPERTS)
    draw_lean = jax.random.randint(key_list[1], (CLIPS, ROWS), 0, EXPERTS)
    offset = jax.random.randint(key_list[2], (CLIPS, 1), 0, EXPERTS)
    first_ids = (draw_base * draw_lean // EXPERTS + offset) % EXPERTS
    priority = jax.vmap(lambda sub: jax.random.permutation(sub, ROWS))(jax.random.split(key_list[3], CLIPS)).astype(jnp.int32)
    first_ids = jnp.where(priority < CAP + 1, offset, first_ids)
    offset_step = jax.random.randint(key_list[4], (CLIPS, ROWS), 1, EXPERTS)
    second = (first_ids + offset_step) % EXPERTS
    id_pairs = jnp.stack([first_ids, second], -1).astype(jnp.int32)
    order_key = (priority[:, :, None] + ROWS * jnp.arange(TOPK, dtype=jnp.int32)[None, None, :]).astype(jnp.int32)

    def clip_rank(ids_of_clip, keys_of_clip):
        flat_ids = ids_of_clip.reshape(-1)
        flat_keys = keys_of_clip.reshape(-1)
        sorted_ids = jnp.zeros((ROWS * TOPK,), jnp.int32).at[flat_keys].set(flat_ids)
        one_hot = (sorted_ids[:, None] == jnp.arange(EXPERTS, dtype=jnp.int32)[None, :]).astype(jnp.int32)
        before = jnp.cumsum(one_hot, 0) - one_hot
        rank_sorted = jnp.sum(before * one_hot, 1)
        return rank_sorted[flat_keys].reshape(ROWS, TOPK)
    ranking = jax.vmap(clip_rank)(id_pairs, order_key).astype(jnp.int32)
    kept = (ranking < CAP).astype(jnp.int32)
    ranking = jnp.minimum(ranking, CAP).astype(jnp.int32)
    return (id_pairs, ranking, kept)


def draw_expert_ids(key, part):
    return route_tables(key)[0]


def draw_priority_ranks(key, part):
    return route_tables(key)[1]


def draw_keep_mask(key, part):
    return route_tables(key)[2]


def shard_levels(own_key, extent, shards, smallest, top_value):
    level = 1.0
    for axis_at, shards_of in shards:
        heights = jax.random.uniform(jax.random.fold_in(jax.random.fold_in(own_key, 6), axis_at), (shards_of,), jnp.float32, smallest / len(shards), top_value / len(shards))
        level = level * jnp.repeat(jnp.exp(heights), extent[axis_at] // shards_of).reshape((-1,) + (1,) * (len(extent) - 1 - axis_at))
    return level


def scatter_about(key, dims, deviation, reach, shards=(), held_as=jnp.bfloat16):
    result = deviation * jax.random.normal(key, dims, jnp.float32)
    if shards:
        result = result * shard_levels(key, dims, shards, -0.22, 0.18)
    return jnp.clip(result, -reach, reach).astype(held_as)


def setup_inputs(seed: int = 0) -> dict:
    streams_of = jax.random.split(jax.random.key(seed), 12)
    return {
        "tokens": scatter_about(streams_of[0], (CLIPS, FRAMES, PATCHES, D), 1.0, 6.0, ((0, 8), (1, 4))),
        "time_taps": scatter_about(streams_of[1], (3, D), 0.6, 3.0, (), jnp.float32),
        "norm_gain": jnp.clip(jax.random.uniform(streams_of[2], (D,), jnp.float32, 0.5, 1.5), 0.5, 1.5),
        "expert_ids": draw_expert_ids(jax.random.fold_in(streams_of[11], 71), 0),
        "priority_ranks": draw_priority_ranks(jax.random.fold_in(streams_of[11], 71), 0),
        "keep_mask": draw_keep_mask(jax.random.fold_in(streams_of[11], 71), 0),
        "gate_weights": jnp.clip(0.2 + 0.8 * jax.random.uniform(streams_of[6], (CLIPS, ROWS, TOPK), jnp.float32) ** shard_levels(streams_of[6], (CLIPS, ROWS, TOPK), ((0, 8),), -0.2, 0.2), 0.2, 1.0),
        "up_weight": scatter_about(streams_of[7], (EXPERTS, D, FF), D ** -0.5, 0.15625, ((0, 8), (2, 4))),
        "down_weight": scatter_about(streams_of[8], (EXPERTS, FF, D), FF ** -0.5, 0.078125, ((0, 8), (1, 4))),
        "attn_gain": jnp.clip(jax.random.uniform(streams_of[9], (D,), jnp.float32, 0.5, 1.5), 0.5, 1.5),
        "qkv_weight": scatter_about(streams_of[10], (3, D, D), D ** -0.5, 0.15625, ((2, 4),)),
    }


eps = 1e-06

def layer_norm(values, gain):
    center = values - lax.optimization_barrier(jnp.mean(values, -1, keepdims=True))
    spread = lax.optimization_barrier(jnp.mean(center * center, -1, keepdims=True))
    return center * lax.rsqrt(spread + eps) * gain

def reference(tokens, time_taps, norm_gain, expert_ids, priority_ranks, keep_mask, gate_weights, up_weight, down_weight, attn_gain, qkv_weight):
    widened = jnp.pad(tokens.astype(jnp.float32), ((0, 0), (2, 0), (0, 0), (0, 0)))
    mixed = (time_taps[0] * widened[:, 2:] + time_taps[1] * widened[:, 1:-1] + time_taps[2] * widened[:, :-2]).astype(jnp.bfloat16)
    clip_rows = mixed.reshape(CLIPS, ROWS, D)
    normed = layer_norm(clip_rows.astype(jnp.float32), norm_gain).astype(jnp.bfloat16)
    slot_index = jnp.where(keep_mask == 1, expert_ids * CAP + priority_ranks, EXPERTS * CAP).astype(jnp.int32)
    token_index = jnp.broadcast_to(jnp.arange(ROWS, dtype=jnp.int32)[:, None], (ROWS, TOPK))

    def build(rows_of_clip, slots_of_clip):
        source = jnp.full((EXPERTS * CAP + 1,), ROWS, jnp.int32).at[slots_of_clip.reshape(-1)].set(token_index.reshape(-1))[:EXPERTS * CAP]
        with_zero = jnp.concatenate([rows_of_clip, jnp.zeros((1, D), jnp.bfloat16)], 0)
        return with_zero[source].reshape(EXPERTS, CAP, D)
    dispatched = jax.vmap(build)(normed, slot_index)

    def expert(packed):
        arrived, up_block, down_block = packed
        flat_rows = arrived.reshape(-1, D)
        hidden = jax.nn.gelu(jnp.dot(flat_rows, up_block, preferred_element_type=jnp.float32)).astype(jnp.bfloat16)
        summed = jnp.zeros((flat_rows.shape[0], D), jnp.float32)
        for portion in range(N_TM):
            lower = portion * FF_DEV
            piece = jnp.dot(hidden[:, lower:lower + FF_DEV], down_block[lower:lower + FF_DEV], preferred_element_type=jnp.float32).astype(jnp.bfloat16)
            summed = summed + lax.optimization_barrier(piece).astype(jnp.float32)
        return summed.astype(jnp.bfloat16).reshape(CLIPS, CAP, D)
    expert_out = lax.map(expert, (jnp.swapaxes(dispatched, 0, 1), up_weight, down_weight))
    expert_out = jnp.swapaxes(expert_out, 0, 1).reshape(CLIPS, EXPERTS * CAP, D)
    table = jnp.concatenate([expert_out, jnp.zeros((CLIPS, 1, D), jnp.bfloat16)], 1)
    picked = jax.vmap(lambda rows_table, slots: rows_table[slots])(table, slot_index)
    weight = jnp.where(keep_mask == 1, gate_weights, 0.0)
    stream = (clip_rows.astype(jnp.float32) + lax.optimization_barrier(jnp.sum(weight[:, :, :, None] * picked.astype(jnp.float32), 2))).astype(jnp.bfloat16)
    attn_in = layer_norm(stream.astype(jnp.float32), attn_gain).astype(jnp.bfloat16)

    def project(rows_of_clip):
        return jnp.stack([jnp.dot(rows_of_clip, qkv_weight[component], preferred_element_type=jnp.float32) for component in range(3)]).astype(jnp.bfloat16)
    qkv_rows = jnp.swapaxes(lax.map(project, attn_in), 0, 1)
    return (stream.reshape(CLIPS, FRAMES, PATCHES, D), qkv_rows)
```

```python
import functools

import jax
import jax.numpy as jnp
from jax import lax
from jax.experimental import pallas as pl
from jax.experimental.pallas import tpu as pltpu
from jax.sharding import PartitionSpec as P

eps = 1e-06
bf16 = jnp.bfloat16
f32 = jnp.float32
ROW_PARTS = 2
VMEM_BYTES = 56 * 1024 * 1024
HBM = pl.BlockSpec(memory_space=pl.ANY)
VMEM = pl.BlockSpec(memory_space=pltpu.VMEM)
SMEM = pl.BlockSpec(memory_space=pltpu.SMEM)


def column_parts(width):
    first = -(-(width // 2) // 128) * 128
    return [(0, first), (first, width - first)]


def call(kernel, out_shape, in_specs, out_specs, scratch, flops, moved, *args):
    return pl.pallas_call(
        kernel,
        out_shape=out_shape,
        in_specs=in_specs,
        out_specs=out_specs,
        scratch_shapes=scratch,
        compiler_params=pltpu.CompilerParams(vmem_limit_bytes=VMEM_BYTES),
        cost_estimate=pl.CostEstimate(flops=flops, bytes_accessed=moved, transcendentals=0),
    )(*args)


def swap(value, axis, distance):
    count = lax.axis_size(axis)
    return lax.ppermute(value, axis, [(i, i ^ distance) for i in range(count)])


def tile_of(rows):
    return 256 if rows % 256 == 0 else rows


def mix_kernel(blocks, patches, where_ref, taps_ref, *refs):
    tokens, mixed_ref, extended, sems = refs[:blocks], refs[-3], refs[-2], refs[-1]
    rows = tokens[0].shape[0]
    halo = 2 * patches
    copies = [
        pltpu.make_async_copy(
            tokens[i],
            extended.at[pl.ds(pl.multiple_of(halo + where_ref[i] * rows, patches), rows)],
            sems.at[i],
        )
        for i in range(blocks)
    ]
    for copy in copies:
        copy.start()
    extended[0:halo] = jnp.zeros((halo, extended.shape[1]), extended.dtype)
    for copy in copies:
        copy.wait()
    tile = patches

    def step(t, carry):
        start = pl.multiple_of(t * tile, tile)
        now = extended[pl.ds(start + halo, tile)].astype(f32)
        before = extended[pl.ds(start + patches, tile)].astype(f32)
        earlier = extended[pl.ds(start, tile)].astype(f32)
        mixed_ref[pl.ds(start, tile)] = (
            taps_ref[0:1] * now + taps_ref[1:2] * before + taps_ref[2:3] * earlier
        ).astype(bf16)
        return carry

    lax.fori_loop(0, blocks * rows // tile, step, 0)


def temporal_mix(tokens, places, taps, patches):
    blocks = len(tokens)
    rows, cols = tokens[0].shape
    total = blocks * rows
    return call(
        functools.partial(mix_kernel, blocks, patches),
        jax.ShapeDtypeStruct((total, cols), bf16),
        [SMEM, VMEM] + [HBM] * blocks,
        VMEM,
        [pltpu.VMEM((total + 2 * patches, cols), bf16), pltpu.SemaphoreType.DMA((blocks,))],
        total * cols * 5,
        total * cols * 4,
        places,
        taps,
        *tokens,
    )


def dispatch_kernel(per, where_ref, slot_ref, mixed_ref, *outs):
    rows = mixed_ref.shape[0]
    me, capacity, first = where_ref[0], where_ref[1], where_ref[2]
    code = slot_ref[...]
    owner = code // capacity
    rank = code - owner * capacity - first
    place = jnp.where((code >= 0) & (rank >= 0) & (rank < per), (owner ^ me) * per + rank, -1)
    together = max(1, 256 // per)
    for base in range(0, len(outs), together):
        group = outs[base : base + together]
        size = per * len(group)
        slots = lax.broadcasted_iota(jnp.int32, (size, rows), 0) + base * per
        hit = (slots == place[0:1]) | (slots == place[1:2])
        picked = jnp.dot(
            jnp.where(hit, 1.0, 0.0).astype(bf16), mixed_ref[...], preferred_element_type=f32
        ).astype(bf16)
        for i, out in enumerate(group):
            out[...] = picked[i * per : (i + 1) * per]


def dispatch(where, slots, mixed, experts, per):
    rows, cols = mixed.shape
    return call(
        functools.partial(dispatch_kernel, per),
        [jax.ShapeDtypeStruct((per, cols), bf16)] * experts,
        [SMEM, VMEM, VMEM],
        [VMEM] * experts,
        [],
        2 * rows * per * experts * cols,
        rows * cols * 2 + experts * per * cols * 2,
        where,
        slots,
        mixed,
    )


def up_kernel(pieces, weights, gain_ref, *refs):
    parts = refs[:pieces]
    ups = refs[pieces : pieces + weights]
    out = refs[pieces + weights]
    rows = parts[0].shape[0]
    tile = tile_of(rows)
    width = gain_ref.shape[1]

    def step(t, carry):
        at = pl.ds(pl.multiple_of(t * tile, tile), tile)
        values = jnp.concatenate([part[at].astype(f32) for part in parts], 1)
        center = values - jnp.sum(values, -1, keepdims=True) * (1.0 / width)
        spread = jnp.sum(center * center, -1, keepdims=True) * (1.0 / width)
        normed = (center * lax.rsqrt(spread + eps) * gain_ref[...]).astype(bf16)
        wide = ups[0].shape[1]
        for i, up in enumerate(ups):
            hidden = jnp.dot(normed, up[...], preferred_element_type=f32)
            out[at, i * wide : (i + 1) * wide] = jax.nn.gelu(hidden).astype(bf16)
        return carry

    lax.fori_loop(0, rows // tile, step, 0)


def up_project(parts, gain, ups):
    rows = parts[0].shape[0]
    wide = sum(up.shape[1] for up in ups)
    width = gain.shape[1]
    return call(
        functools.partial(up_kernel, len(parts), len(ups)),
        jax.ShapeDtypeStruct((rows, wide), bf16),
        [VMEM] * (1 + len(parts) + len(ups)),
        VMEM,
        [],
        2 * rows * width * wide,
        rows * (width + wide) * 2 + width * wide * 2,
        gain,
        *parts,
        *ups,
    )


def down_kernel(pieces, weights, blocks, *refs):
    hiddens = refs[:pieces]
    downs = refs[pieces : pieces + weights * blocks]
    outs = refs[pieces + weights * blocks :]
    base = 0
    for hidden in hiddens:
        rows = hidden.shape[0]
        tile = tile_of(rows)

        def step(t, carry, hidden=hidden, base=base, tile=tile):
            start = t * tile
            for d in range(blocks):
                deep = downs[d].shape[0]
                total = 0.0
                for i in range(weights):
                    total = total + jnp.dot(
                        hidden[
                            pl.ds(pl.multiple_of(start, tile), tile), i * deep : (i + 1) * deep
                        ],
                        downs[i * blocks + d][...],
                        preferred_element_type=f32,
                    )
                outs[d][pl.ds(pl.multiple_of(base + start, tile), tile)] = total.astype(bf16)
            return carry

        lax.fori_loop(0, rows // tile, step, 0)
        base += rows


def down_project(hiddens, downs):
    rows = sum(hidden.shape[0] for hidden in hiddens)
    blocks = len(downs[0])
    deep, cols = downs[0][0].shape
    flat = [block for group in downs for block in group]
    return call(
        functools.partial(down_kernel, len(hiddens), len(downs), blocks),
        [jax.ShapeDtypeStruct((rows, cols), bf16)] * blocks,
        [VMEM] * (len(hiddens) + len(flat)),
        [VMEM] * blocks,
        [],
        2 * rows * deep * len(downs) * cols * blocks,
        rows * deep * len(downs) * 2 + deep * len(downs) * cols * blocks * 2,
        *hiddens,
        *flat,
    )


def sum_kernel(pieces, parts, per, *refs):
    values, outs = refs[:pieces], refs[pieces:]
    experts = len(outs)
    for k, out in enumerate(outs):
        for h in range(parts):
            at = slice((h * experts + k) * per, (h * experts + k + 1) * per)
            total = values[0][at].astype(f32)
            for value in values[1:]:
                total = total + value[at].astype(f32)
            out[h * per : (h + 1) * per] = total.astype(bf16)


def sum_blocks(values, experts, parts, per):
    rows, cols = values[0].shape
    return call(
        functools.partial(sum_kernel, len(values), parts, per),
        [jax.ShapeDtypeStruct((parts * per, cols), bf16)] * experts,
        [VMEM] * len(values),
        [VMEM] * experts,
        [],
        rows * cols * 2,
        rows * cols * 2 * (len(values) + 1),
        *values,
    )


def combine_kernel(tables, first_col, where_ref, slot_ref, gate_ref, mixed_ref, *refs):
    sources, out, base, table, sems, base_sems = refs[:tables], *refs[tables:]
    cols = out.shape[1]
    blocks = where_ref.shape[0] - 3
    rows = out.shape[0] // blocks
    copies = []
    for i in range(blocks):
        start = pl.multiple_of(where_ref[3 + i] * rows, rows)
        copies.append(
            pltpu.make_async_copy(
                mixed_ref.at[pl.ds(start, rows), first_col : first_col + cols],
                base.at[i * rows : (i + 1) * rows],
                base_sems.at[i],
            )
        )
    many = sources[0].shape[0]
    for i, source in enumerate(sources):
        copies.append(
            pltpu.make_async_copy(source, table.at[i * many : (i + 1) * many], sems.at[i])
        )
    for copy in copies:
        copy.start()
    me, capacity, core = where_ref[0], where_ref[1], where_ref[2]
    half = capacity // tables
    slots = tables * many
    for copy in copies:
        copy.wait()
    tile = tile_of(out.shape[0])

    def step(t, carry):
        at = pl.ds(pl.multiple_of(t * tile, tile), tile)
        code = slot_ref[at]
        owner = code // capacity
        rank = code - owner * capacity
        part = rank // half
        place = jnp.where(
            code >= 0, (part ^ core) * many + (owner ^ me) * half + rank - part * half, -1
        )
        total = base[at].astype(f32)
        added = jnp.zeros((tile, cols), f32)
        lanes = lax.broadcasted_iota(jnp.int32, (tile, slots), 1)
        for k in range(code.shape[1]):
            hit = jnp.where(lanes == place[:, k : k + 1], 1.0, 0.0).astype(bf16)
            picked = jnp.dot(hit, table[...], preferred_element_type=f32)
            added = added + gate_ref[at, k : k + 1] * picked
        out[at] = (total + added).astype(bf16)
        return carry

    lax.fori_loop(0, out.shape[0] // tile, step, 0)


def combine(where, slots, gates, mixed, sources, first_col):
    blocks = where.shape[0] - 3
    rows = slots.shape[0]
    many, cols = sources[0].shape
    tables = len(sources)
    return call(
        functools.partial(combine_kernel, tables, first_col),
        jax.ShapeDtypeStruct((rows, cols), bf16),
        [SMEM, VMEM, VMEM, HBM] + [HBM] * tables,
        VMEM,
        [
            pltpu.VMEM((rows, cols), bf16),
            pltpu.VMEM((tables * many, cols), bf16),
            pltpu.SemaphoreType.DMA((tables,)),
            pltpu.SemaphoreType.DMA((blocks,)),
        ],
        4 * rows * many * tables * cols,
        rows * cols * 4 + tables * many * cols * 2,
        where,
        slots,
        gates,
        mixed,
        *sources,
    )


def qkv_kernel(groups, pieces, blocks, where_ref, gain_ref, weight_ref, *refs):
    streams, out = refs[: groups * pieces], refs[groups * pieces]
    rows = streams[0].shape[0] // blocks
    width = gain_ref.shape[1]
    tile = tile_of(rows)
    per = rows // tile
    heads = out.shape[2]

    for g in range(groups):

        def step(t, carry, g=g):
            block = t // per
            at = pl.ds(pl.multiple_of(t * tile, tile), tile)
            values = jnp.concatenate(
                [streams[g * pieces + i][at].astype(f32) for i in range(pieces)], 1
            )
            center = values - jnp.sum(values, -1, keepdims=True) * (1.0 / width)
            spread = jnp.sum(center * center, -1, keepdims=True) * (1.0 / width)
            normed = (center * lax.rsqrt(spread + eps) * gain_ref[...]).astype(bf16)
            result = jnp.dot(normed, weight_ref[...], preferred_element_type=f32).astype(bf16)
            start = where_ref[g * blocks + block] * rows + (t - block * per) * tile
            to = pl.ds(pl.multiple_of(start, tile), tile)
            for j in range(out.shape[0]):
                out[j, to] = result[:, j * heads : (j + 1) * heads]
            return carry

        lax.fori_loop(0, blocks * per, step, 0)


def qkv_project(where, gain, weight, streams, blocks):
    groups, pieces = len(streams), len(streams[0])
    flat = [piece for group in streams for piece in group]
    rows = sum(group[0].shape[0] for group in streams)
    width, wide = weight.shape
    return call(
        functools.partial(qkv_kernel, groups, pieces, blocks),
        jax.ShapeDtypeStruct((3, rows, wide // 3), bf16),
        [SMEM, VMEM, VMEM] + [VMEM] * len(flat),
        VMEM,
        [],
        2 * rows * width * wide,
        rows * (width + wide) * 2 + width * wide * 2,
        where,
        gain,
        weight,
        *flat,
    )


def local(
    tokens,
    time_taps,
    norm_gain,
    expert_ids,
    priority_ranks,
    keep_mask,
    gate_weights,
    up_weight,
    down_weight,
    attn_gain,
    qkv_weight,
):
    frames_here, patches, width = tokens.shape[1:]
    members = lax.axis_size("tm")
    experts = lax.axis_size("expert")
    chips = members // 2
    cols = width // chips
    place = lax.axis_index("tm")
    chip, core = place // 2, place % 2
    me = lax.axis_index("expert")
    own_rows = frames_here * patches
    rows = own_rows * members
    capacity = rows * expert_ids.shape[2] // (2 * experts)
    half = capacity // 2
    per = half // ROW_PARTS
    parts = column_parts(cols)

    def columns_of(value, d, at=0, size=cols):
        return lax.dynamic_slice_in_dim(value, (chip ^ d) * cols + at, size, value.ndim - 1)

    def by_share(value):
        return jnp.concatenate(
            [lax.dynamic_slice_in_dim(value, (chip ^ d) * cols, cols, 0) for d in range(chips)], 0
        )

    own_tokens = tokens.reshape(own_rows, width)
    mine = columns_of(own_tokens, 0)
    near = [mine] + [swap(columns_of(own_tokens, d), "tm", 2 * d) for d in range(1, chips)]
    over = [swap(value, "tm", 1) for value in near]
    near_places = [(chip ^ d) * 2 + core for d in range(chips)]
    over_places = [(chip ^ d) * 2 + 1 - core for d in range(chips)]

    up_mine = by_share(up_weight[0])
    ups = [up_mine, swap(up_mine, "tm", 1)]
    downs = []
    for at, size in parts:
        group = [columns_of(down_weight[0], d, at, size) for d in range(chips)]
        downs.append([group, [swap(block, "tm", 1) for block in group]])
    gain_up = by_share(norm_gain)[None]
    gain_qkv = by_share(attn_gain)[None]
    qkv_mine = by_share(jnp.swapaxes(qkv_weight, 0, 1).reshape(width, -1))
    taps = columns_of(time_taps, 0)

    code = jnp.where(keep_mask[0] == 1, expert_ids[0] * capacity + priority_ranks[0], -1)
    token_places = jnp.stack(near_places + over_places).astype(jnp.int32)
    mixed = temporal_mix(near + over, token_places, taps, patches)

    code_rows = code.T
    hiddens = []
    for h in range(ROW_PARTS):
        where = jnp.stack([me, jnp.int32(capacity), core * half + h * per]).astype(jnp.int32)
        blocks = dispatch(where, code_rows, mixed, experts, per)
        arrived = jnp.concatenate(
            [blocks[0]] + [swap(blocks[k], "expert", k) for k in range(1, experts)], 0
        )
        shares = [arrived] + [swap(arrived, "tm", 2 * d) for d in range(1, chips)]
        hiddens.append(up_project(shares, gain_up, ups))

    block_places = jnp.stack([i * 2 + core for i in range(chips)]).astype(jnp.int32)
    where = jnp.concatenate(
        [jnp.stack([me, jnp.int32(capacity), core]).astype(jnp.int32), block_places]
    )

    def rows_of(value):
        shaped = value.reshape(chips, 2, own_rows, -1)
        return lax.dynamic_index_in_dim(shaped, core, 1, keepdims=False).reshape(
            chips * own_rows, -1
        )

    code_here = rows_of(code)
    gates_here = rows_of(gate_weights[0])
    here = [[None] * len(parts) for _ in range(chips)]
    there = [[None] * len(parts) for _ in range(chips)]
    for q, (at, size) in enumerate(parts):
        sums = down_project(hiddens, downs[q])
        pieces = [sums[0]] + [swap(sums[d], "tm", 2 * d) for d in range(1, chips)]
        outgoing = sum_blocks(pieces, experts, ROW_PARTS, per)
        returned = jnp.concatenate(
            [outgoing[0]] + [swap(outgoing[k], "expert", k) for k in range(1, experts)], 0
        )
        tables = [returned, swap(returned, "tm", 1)]
        stream = combine(where, code_here, gates_here, mixed, tables, at)
        for d in range(chips):
            here[d][q] = stream if d == 0 else swap(stream, "tm", 2 * d)
            there[d][q] = swap(here[d][q], "tm", 1)

    streams = [sum(here, []), sum(there, [])]
    order = jnp.stack(
        [i * 2 + core for i in range(chips)] + [i * 2 + 1 - core for i in range(chips)]
    ).astype(jnp.int32)
    qkv_rows = qkv_project(order, gain_qkv, qkv_mine, streams, chips)[:, None]

    own = [
        jnp.concatenate(
            [lax.dynamic_slice_in_dim(v, chip * own_rows, own_rows, 0) for v in here[d]], 1
        )
        for d in range(chips)
    ]
    stacked = jnp.stack(own)
    stream_here = jnp.concatenate([stacked[chip ^ i] for i in range(chips)], 1)
    return (stream_here.reshape(tokens.shape), qkv_rows)


def solution(mesh):
    in_specs = (
        P("expert", "tm", None, None),
        P(),
        P(),
        P("expert", None, None),
        P("expert", None, None),
        P("expert", None, None),
        P("expert", None, None),
        P("expert", None, "tm"),
        P("expert", "tm", None),
        P(),
        P(None, None, "tm"),
    )
    out_specs = (P("expert", "tm", None, None), P(None, "expert", None, "tm"))
    return jax.shard_map(local, mesh=mesh, in_specs=in_specs, out_specs=out_specs, check_vma=False)
```

```python
import functools

import jax
import jax.numpy as jnp
from jax import lax
from jax.experimental import pallas as pl
from jax.experimental.pallas import tpu as pltpu
from jax.sharding import PartitionSpec as P

eps = 1e-06
bf16 = jnp.bfloat16
f32 = jnp.float32
HBM = pl.BlockSpec(memory_space=pl.ANY)
VMEM = pl.BlockSpec(memory_space=pltpu.VMEM)
SMEM = pl.BlockSpec(memory_space=pltpu.SMEM)


def call(kernel, out_shape, in_specs, out_specs, scratch, megabytes, flops, moved, *args):
    return pl.pallas_call(
        kernel,
        out_shape=out_shape,
        in_specs=in_specs,
        out_specs=out_specs,
        scratch_shapes=scratch,
        compiler_params=pltpu.CompilerParams(vmem_limit_bytes=megabytes << 20),
        cost_estimate=pl.CostEstimate(flops=flops, bytes_accessed=moved, transcendentals=0),
    )(*args)


def swap(value, axis, distance):
    count = lax.axis_size(axis)
    return lax.ppermute(value, axis, [(i, i ^ distance) for i in range(count)])


def tile_of(rows, most=512):
    return most if rows % most == 0 else rows


def mix_kernel(blocks, patches, where_ref, taps_ref, *refs):
    tokens, mixed_ref, extended, sems = refs[:blocks], refs[-3], refs[-2], refs[-1]
    rows = tokens[0].shape[0]
    copies = [
        pltpu.make_async_copy(
            tokens[i],
            extended.at[pl.ds(pl.multiple_of(where_ref[i] * rows, rows), rows)],
            sems.at[i],
        )
        for i in range(blocks)
    ]
    for copy in copies:
        copy.start()
    for copy in copies:
        copy.wait()
    frames = blocks * rows // patches
    width = extended.shape[1]
    for left in range(0, width, 128):
        lanes = slice(left, min(left + 128, width))
        taps = [taps_ref[i : i + 1, lanes] for i in range(3)]

        def step(t, carry, lanes=lanes, taps=taps):
            earlier, before = carry
            start = pl.multiple_of(t * patches, patches)
            now = extended[pl.ds(start, patches), lanes].astype(f32)
            mixed = taps[0] * now + taps[1] * before + taps[2] * earlier
            mixed_ref[pl.ds(start, patches), lanes] = mixed.astype(bf16)
            return before, now

        first = extended[0:patches, lanes].astype(f32)
        second = extended[patches : 2 * patches, lanes].astype(f32)
        mixed_ref[0:patches, lanes] = (taps[0] * first).astype(bf16)
        mixed_ref[patches : 2 * patches, lanes] = (taps[0] * second + taps[1] * first).astype(bf16)
        lax.fori_loop(2, frames, step, (first, second), unroll=3)


def temporal_mix(tokens, places, taps, patches):
    blocks = len(tokens)
    rows, cols = tokens[0].shape
    total = blocks * rows
    return call(
        functools.partial(mix_kernel, blocks, patches),
        jax.ShapeDtypeStruct((total, cols), bf16),
        [SMEM, VMEM] + [HBM] * blocks,
        VMEM,
        [pltpu.VMEM((total, cols), bf16), pltpu.SemaphoreType.DMA((blocks,))],
        16,
        total * cols * 5,
        total * cols * 4,
        places,
        taps,
        *tokens,
    )


def dispatch_kernel(per, place_ref, mixed_ref, *outs):
    rows = mixed_ref.shape[0]
    place = place_ref[...]
    together = max(1, 512 // per)
    for base in range(0, len(outs), together):
        group = outs[base : base + together]
        size = per * len(group)
        slots = lax.broadcasted_iota(jnp.int32, (size, rows), 0) + base * per
        hit = (slots == place[0:1]) | (slots == place[1:2])
        picked = jnp.dot(
            jnp.where(hit, 1.0, 0.0).astype(bf16), mixed_ref[...], preferred_element_type=f32
        ).astype(bf16)
        for i, out in enumerate(group):
            out[...] = picked[i * per : (i + 1) * per]


def dispatch(place, mixed, experts, per):
    rows, cols = mixed.shape
    return call(
        functools.partial(dispatch_kernel, per),
        [jax.ShapeDtypeStruct((per, cols), bf16)] * experts,
        [VMEM, VMEM],
        [VMEM] * experts,
        [],
        24,
        2 * rows * per * experts * cols,
        rows * cols * 2 + experts * per * cols * 2,
        place,
        mixed,
    )


def normalised(values, gain):
    scale = 1.0 / values.shape[1]
    center = values - jnp.sum(values, -1, keepdims=True) * scale
    spread = jnp.sum(center * center, -1, keepdims=True) * scale
    return (center * lax.rsqrt(spread + eps) * gain).astype(bf16)


def in_order(chip, shares, run):
    for i in range(shares):

        @pl.when(chip == i)
        def _(i=i):
            run([i ^ j for j in range(shares)])


def expert_kernel(shares, where_ref, gain_ref, *refs):
    parts, refs = refs[:shares], refs[shares:]
    weights, refs = refs[:4], refs[4:]
    outs, refs = refs[:shares], refs[shares:]
    normed, hidden, held, sems = refs[0], refs[1], refs[2:6], refs[6]
    rows, cols = parts[0].shape
    copies = [
        pltpu.make_async_copy(weight, place, sems.at[i])
        for i, (weight, place) in enumerate(zip(weights, held))
    ]
    for copy in copies:
        copy.start()
    tile = tile_of(rows, 256)

    def norm(order):
        for at in range(0, rows, tile):
            values = jnp.concatenate(
                [parts[d][at : at + tile].astype(f32) for d in order], 1
            )
            normed[at : at + tile] = normalised(values, gain_ref[...])

    in_order(where_ref[0], shares, norm)
    ups, downs = held[:2], held[2:]
    wide = ups[0].shape[1]
    step = 256 if wide % 256 == 0 else wide
    for i, up in enumerate(ups):
        copies[i].wait()
        for left in range(0, wide, step):
            product = jnp.dot(normed[...], up[:, left : left + step], preferred_element_type=f32)
            at = i * wide + left
            hidden[:, at : at + step] = jax.nn.gelu(product).astype(bf16)
    for copy in copies[2:]:
        copy.wait()
    for j in range(shares):
        at = slice(j * cols, (j + 1) * cols)
        total = jnp.dot(hidden[:, :wide], downs[0][:, at], preferred_element_type=f32)
        total += jnp.dot(hidden[:, wide:], downs[1][:, at], preferred_element_type=f32)
        result = total.astype(bf16)

        def store(order, j=j, result=result):
            outs[order[j]][...] = result

        in_order(where_ref[0], shares, store)


def expert_project(where, gain, parts, ups, downs):
    rows, cols = parts[0].shape
    shares = len(parts)
    width, wide = ups[0].shape
    return call(
        functools.partial(expert_kernel, shares),
        [jax.ShapeDtypeStruct((rows, cols), bf16)] * shares,
        [SMEM, VMEM] + [VMEM] * shares + [HBM] * 4,
        [VMEM] * shares,
        [
            pltpu.VMEM((rows, width), bf16),
            pltpu.VMEM((rows, 2 * wide), bf16),
            pltpu.VMEM((width, wide), bf16),
            pltpu.VMEM((width, wide), bf16),
            pltpu.VMEM((wide, width), bf16),
            pltpu.VMEM((wide, width), bf16),
            pltpu.SemaphoreType.DMA((4,)),
        ],
        28,
        8 * rows * width * wide,
        8 * width * wide + rows * width * 4,
        where,
        gain,
        *parts,
        *ups,
        *downs,
    )


def sum_kernel(pieces, *refs):
    values, outs = refs[:pieces], refs[pieces:]
    rows = outs[0].shape[0]
    for i, out in enumerate(outs):
        at = slice(i * rows, (i + 1) * rows)
        total = values[0][at].astype(f32)
        for value in values[1:]:
            total = total + value[at].astype(f32)
        out[...] = total.astype(bf16)


def sum_blocks(values, blocks):
    rows, cols = values[0].shape
    return call(
        functools.partial(sum_kernel, len(values)),
        [jax.ShapeDtypeStruct((rows // blocks, cols), bf16)] * blocks,
        [VMEM] * len(values),
        [VMEM] * blocks,
        [],
        8,
        rows * cols * 2,
        rows * cols * 2 * (len(values) + 1),
        *values,
    )


def combine_kernel(tables, where_ref, place_ref, gate_ref, mixed_ref, *refs):
    sources, out = refs[:tables], refs[tables]
    rows = out.shape[0]
    start = pl.multiple_of(where_ref[0] * rows, rows)
    total = mixed_ref[pl.ds(start, rows)].astype(f32)
    place, gate = place_ref[...], gate_ref[...]
    first = 0
    for source in sources:
        many = source.shape[0]
        lanes = lax.broadcasted_iota(jnp.int32, (rows, many), 1) + first
        weight = jnp.zeros((rows, many), f32)
        for k in range(place.shape[1]):
            weight = jnp.where(lanes == place[:, k : k + 1], gate[:, k : k + 1], weight)
        total = total + jnp.dot(weight.astype(bf16), source[...], preferred_element_type=f32)
        first += many
    out[...] = total.astype(bf16)


def combine(where, places, gates, mixed, sources):
    rows, cols = places.shape[0], mixed.shape[1]
    many = sum(source.shape[0] for source in sources)
    return call(
        functools.partial(combine_kernel, len(sources)),
        jax.ShapeDtypeStruct((rows, cols), bf16),
        [SMEM, VMEM, VMEM, VMEM] + [VMEM] * len(sources),
        VMEM,
        [],
        20,
        2 * rows * many * cols,
        rows * cols * 4 + many * cols * 2,
        where,
        places,
        gates,
        mixed,
        *sources,
    )


def qkv_kernel(shares, where_ref, gain_ref, weight_ref, *refs):
    parts, out, normed, held, sem = refs[:shares], *refs[-4:]
    rows = parts[0].shape[0]
    heads = out.shape[1]

    def norm(order):
        values = jnp.concatenate([parts[d][...].astype(f32) for d in order], 1)
        normed[...] = normalised(values, gain_ref[...])

    in_order(where_ref[0], shares, norm)
    to = pl.ds(pl.multiple_of(where_ref[1] * rows, rows), rows)
    copies = []
    for j in range(out.shape[0]):
        result = lax.dot_general(
            weight_ref[j * heads : (j + 1) * heads],
            normed[...],
            (((1,), (1,)), ((), ())),
            preferred_element_type=f32,
        )
        held[j] = result.astype(bf16)
        copies.append(pltpu.make_async_copy(held.at[j], out.at[j, :, to], sem.at[j]))
        copies[-1].start()
    for copy in copies:
        copy.wait()


def qkv_project(where, gain, weight, parts, total, earlier):
    shares = len(parts)
    rows = parts[0].shape[0]
    wide, width = weight.shape
    inputs = [where, gain, weight, *parts] + ([] if earlier is None else [earlier])
    return pl.pallas_call(
        functools.partial(qkv_kernel, shares),
        out_shape=jax.ShapeDtypeStruct((3, wide // 3, total), bf16),
        in_specs=[SMEM, VMEM, VMEM] + [VMEM] * shares + [HBM] * (earlier is not None),
        out_specs=HBM,
        scratch_shapes=[
            pltpu.VMEM((rows, width), bf16),
            pltpu.VMEM((3, wide // 3, rows), bf16),
            pltpu.SemaphoreType.DMA((3,)),
        ],
        input_output_aliases={} if earlier is None else {3 + shares: 0},
        compiler_params=pltpu.CompilerParams(vmem_limit_bytes=20 << 20),
        cost_estimate=pl.CostEstimate(
            flops=2 * rows * width * wide,
            bytes_accessed=rows * (width + wide) * 2 + width * wide * 2,
            transcendentals=0,
        ),
    )(*inputs)


def local(
    tokens,
    time_taps,
    norm_gain,
    expert_ids,
    priority_ranks,
    keep_mask,
    gate_weights,
    up_weight,
    down_weight,
    attn_gain,
    qkv_weight,
):
    frames_here, patches, width = tokens.shape[1:]
    members = lax.axis_size("tm")
    experts = lax.axis_size("expert")
    chips = members // 2
    cols = width // chips
    place = lax.axis_index("tm")
    chip, core = place // 2, place % 2
    me = lax.axis_index("expert")
    own_rows = frames_here * patches
    rows = own_rows * members
    capacity = rows * expert_ids.shape[2] // (2 * experts)
    half = capacity // 2

    def columns_of(value, d):
        return lax.dynamic_slice_in_dim(value, (chip ^ d) * cols, cols, value.ndim - 1)

    def rows_of(value, i):
        return lax.dynamic_slice_in_dim(value, (2 * i + core) * own_rows, own_rows, 0)

    own_tokens = tokens.reshape(own_rows, width)
    mine = columns_of(own_tokens, 0)
    near = [mine] + [swap(columns_of(own_tokens, d), "tm", 2 * d) for d in range(1, chips)]
    over = [swap(value, "tm", 1) for value in near]
    token_places = jnp.stack(
        [(chip ^ d) * 2 + core for d in range(chips)]
        + [(chip ^ d) * 2 + 1 - core for d in range(chips)]
    ).astype(jnp.int32)

    ups = [up_weight[0], swap(up_weight[0], "tm", 1)]
    downs = [down_weight[0], swap(down_weight[0], "tm", 1)]
    qkv_columns = jnp.swapaxes(qkv_weight, 1, 2).reshape(-1, width)
    taps = columns_of(time_taps, 0)

    ids, ranks, kept = expert_ids[0], priority_ranks[0], keep_mask[0] == 1
    here_first = core * half
    out_place = jnp.where(
        kept & (ranks >= here_first) & (ranks < here_first + half),
        (ids ^ me) * half + ranks - here_first,
        -1,
    ).T
    upper = (ranks >= half).astype(jnp.int32)
    back_place = jnp.where(
        kept, ((upper ^ core) * experts + (ids ^ me)) * half + ranks - upper * half, -1
    )
    places = [rows_of(back_place, i) for i in range(chips)]
    gates = [rows_of(gate_weights[0], i) for i in range(chips)]
    where_chip = chip.astype(jnp.int32)[None]

    near, over, ups, downs, out_place, places, gates = lax.optimization_barrier(
        (near, over, ups, downs, out_place, places, gates)
    )
    mixed = temporal_mix(near + over, token_places, taps, patches)

    middle = experts // 2
    far = dispatch(out_place - middle * half, mixed, experts - middle, half)
    close = dispatch(out_place, mixed, middle, half)
    sent = list(close) + list(far)
    arrived = [sent[0]] + [swap(sent[k], "expert", k) for k in range(1, experts)]
    bounds = [0, middle, middle + middle // 2, experts]
    groups = [range(*pair) for pair in zip(bounds, bounds[1:])]
    partial_sums = []
    for group in groups:
        rows_in = jnp.concatenate([arrived[k] for k in group], 0)
        shares = [rows_in] + [swap(rows_in, "tm", 2 * d) for d in range(1, chips)]
        partial_sums.append(expert_project(where_chip, norm_gain[None], shares, ups, downs))

    back = [None] * len(groups)
    for g in (1, 2, 0):
        sums = partial_sums[g]
        pieces = [sums[0]] + [swap(sums[d], "tm", 2 * d) for d in range(1, chips)]
        blocks = sum_blocks(pieces, len(groups[g]))
        back[g] = jnp.concatenate(
            [swap(block, "expert", k) if k else block for k, block in zip(groups[g], blocks)], 0
        )
    sources = back + [swap(value, "tm", 1) for value in back]

    stream = []
    for i in range(chips):
        block = (2 * i + core).astype(jnp.int32)[None]
        stream.append(combine(block, places[i], gates[i], mixed, sources))
    qkv_rows = None
    full = []
    for i in range(chips):
        pieces = [stream[i]] + [swap(stream[i], "tm", 2 * d) for d in range(1, chips)]
        full.append(pieces)
        other = [swap(piece, "tm", 1) for piece in pieces]
        for side, parts in ((core, pieces), (1 - core, other)):
            where = jnp.stack([chip, 2 * i + side]).astype(jnp.int32)
            qkv_rows = qkv_project(where, attn_gain[None], qkv_columns, parts, rows, qkv_rows)

    stacked = jnp.stack(
        [jnp.where(chip == 0, full[0][d], full[1][d]) for d in range(chips)]
        if chips == 2
        else [jnp.stack([full[i][d] for i in range(chips)])[chip] for d in range(chips)]
    )
    stream_here = jnp.concatenate([stacked[chip ^ i] for i in range(chips)], 1)
    return (stream_here.reshape(tokens.shape), jnp.swapaxes(qkv_rows, 1, 2)[:, None])


def solution(mesh):
    in_specs = (
        P("expert", "tm", None, None),
        P(),
        P(),
        P("expert", None, None),
        P("expert", None, None),
        P("expert", None, None),
        P("expert", None, None),
        P("expert", None, "tm"),
        P("expert", "tm", None),
        P(),
        P(None, None, "tm"),
    )
    out_specs = (P("expert", "tm", None, None), P(None, "expert", None, "tm"))
    return jax.shard_map(local, mesh=mesh, in_specs=in_specs, out_specs=out_specs, check_vma=False)
```

```python
import functools

import jax
import jax.numpy as jnp
from jax import lax
from jax.experimental import pallas as pl
from jax.experimental.pallas import tpu as pltpu
from jax.sharding import PartitionSpec as P

eps = 1e-06
bf16 = jnp.bfloat16
f32 = jnp.float32
HBM = pl.BlockSpec(memory_space=pl.ANY)
VMEM = pl.BlockSpec(memory_space=pltpu.VMEM)
SMEM = pl.BlockSpec(memory_space=pltpu.SMEM)


def call(kernel, out_shape, in_specs, out_specs, scratch, megabytes, flops, moved, *args):
    return pl.pallas_call(
        kernel,
        out_shape=out_shape,
        in_specs=in_specs,
        out_specs=out_specs,
        scratch_shapes=scratch,
        compiler_params=pltpu.CompilerParams(vmem_limit_bytes=megabytes << 20),
        cost_estimate=pl.CostEstimate(flops=flops, bytes_accessed=moved, transcendentals=0),
    )(*args)


def swap(value, axis, distance):
    count = lax.axis_size(axis)
    return lax.ppermute(value, axis, [(i, i ^ distance) for i in range(count)])


def after(value, *others):
    return lax.optimization_barrier((value, others))[0]


def tile_of(rows, most=512):
    return most if rows % most == 0 else rows


def places_kernel(half, experts, where_ref, ids_ref, ranks_ref, keep_ref, gate_ref, out_ref, back_ref):
    me, core = where_ref[0], where_ref[1]
    ids, ranks, kept = ids_ref[...] ^ me, ranks_ref[...], keep_ref[...] == 1
    own = ranks - core * half
    out_ref[...] = jnp.where(kept & (own >= 0) & (own < half), ids * half + own, -1)
    upper = jnp.where(ranks >= half, 1, 0)
    back = ((upper ^ core) * experts + ids) * half + ranks - upper * half
    table = [jnp.where(kept, back, -1).astype(f32), gate_ref[...]]
    filler = jnp.zeros((8 - 2 * ids.shape[0], ids.shape[1]), f32)
    back_ref[...] = jnp.concatenate(table + [filler], 0).T


def slot_places(where, ids, ranks, keep, gates, half, experts):
    choices, rows = ids.shape
    return call(
        functools.partial(places_kernel, half, experts),
        [
            jax.ShapeDtypeStruct((choices, rows), jnp.int32),
            jax.ShapeDtypeStruct((rows, 8), f32),
        ],
        [SMEM] + [VMEM] * 4,
        [VMEM] * 2,
        [],
        8,
        rows * 64,
        rows * 512,
        where,
        ids,
        ranks,
        keep,
        gates,
    )


def dispatch_kernel(blocks, patches, per, where_ref, taps_ref, place_ref, *refs):
    tokens, refs = refs[:blocks], refs[blocks:]
    base_ref, outs, (extended, mixed_ref, sems) = refs[0], refs[1:-3], refs[-3:]
    rows = tokens[0].shape[0]
    copies = [
        pltpu.make_async_copy(
            tokens[i],
            extended.at[pl.ds(pl.multiple_of(where_ref[i] * rows, rows), rows)],
            sems.at[i],
        )
        for i in range(blocks)
    ]
    for copy in copies:
        copy.start()
    for copy in copies:
        copy.wait()
    frames = blocks * rows // patches
    width = extended.shape[1]
    for left in range(0, width, 128):
        lanes = slice(left, min(left + 128, width))
        taps = [taps_ref[i : i + 1, lanes] for i in range(3)]

        def step(t, carry, lanes=lanes, taps=taps):
            earlier, before = carry
            start = pl.multiple_of(t * patches, patches)
            now = extended[pl.ds(start, patches), lanes].astype(f32)
            mixed = taps[0] * now + taps[1] * before + taps[2] * earlier
            mixed_ref[pl.ds(start, patches), lanes] = mixed.astype(bf16)
            return before, now

        first = extended[0:patches, lanes].astype(f32)
        second = extended[patches : 2 * patches, lanes].astype(f32)
        mixed_ref[0:patches, lanes] = (taps[0] * first).astype(bf16)
        mixed_ref[patches : 2 * patches, lanes] = (taps[0] * second + taps[1] * first).astype(bf16)
        lax.fori_loop(2, frames, step, (first, second), unroll=3)

    place = place_ref[...]
    together = max(1, 512 // per)
    for base in range(0, len(outs), together):
        group = outs[base : base + together]
        size = per * len(group)
        slots = lax.broadcasted_iota(jnp.int32, (size, blocks * rows), 0) + base * per
        hit = (slots == place[0:1]) | (slots == place[1:2])
        picked = jnp.dot(
            jnp.where(hit, 1.0, 0.0).astype(bf16), mixed_ref[...], preferred_element_type=f32
        ).astype(bf16)
        for i, out in enumerate(group):
            out[...] = picked[i * per : (i + 1) * per]
    for i in range(blocks // 2):
        start = pl.multiple_of(where_ref[blocks + i] * rows, rows)
        base_ref[i * rows : (i + 1) * rows] = mixed_ref[pl.ds(start, rows)]


def mix_and_dispatch(where, taps, place, tokens, patches, experts, per):
    blocks = len(tokens)
    rows, cols = tokens[0].shape
    total = blocks * rows
    return call(
        functools.partial(dispatch_kernel, blocks, patches, per),
        [jax.ShapeDtypeStruct((total // 2, cols), bf16)]
        + [jax.ShapeDtypeStruct((per, cols), bf16)] * experts,
        [SMEM, VMEM, VMEM] + [HBM] * blocks,
        [VMEM] * (1 + experts),
        [
            pltpu.VMEM((total, cols), bf16),
            pltpu.VMEM((total, cols), bf16),
            pltpu.SemaphoreType.DMA((blocks,)),
        ],
        24,
        2 * total * per * experts * cols,
        total * cols * 2 + experts * per * cols * 2,
        where,
        taps,
        place,
        *tokens,
    )


def normalised(values, gain):
    scale = 1.0 / values.shape[1]
    center = values - jnp.sum(values, -1, keepdims=True) * scale
    spread = jnp.sum(center * center, -1, keepdims=True) * scale
    return (center * lax.rsqrt(spread + eps) * gain).astype(bf16)


def in_order(chip, shares, run):
    for i in range(shares):

        @pl.when(chip == i)
        def _(i=i):
            run([i ^ j for j in range(shares)])


def expert_kernel(shares, where_ref, gain_ref, *refs):
    parts, refs = refs[:shares], refs[shares:]
    weights, refs = refs[:4], refs[4:]
    outs, refs = refs[:shares], refs[shares:]
    normed, hidden, held, sems = refs[0], refs[1], refs[2:6], refs[6]
    rows, cols = parts[0].shape
    copies = [
        pltpu.make_async_copy(weight, place, sems.at[i])
        for i, (weight, place) in enumerate(zip(weights, held))
    ]
    for copy in copies:
        copy.start()
    tile = tile_of(rows, 256)

    def norm(order):
        for at in range(0, rows, tile):
            values = jnp.concatenate(
                [parts[d][at : at + tile].astype(f32) for d in order], 1
            )
            normed[at : at + tile] = normalised(values, gain_ref[...])

    in_order(where_ref[0], shares, norm)
    ups, downs = held[:2], held[2:]
    wide = ups[0].shape[1]
    step = 256 if wide % 256 == 0 else wide
    for i, up in enumerate(ups):
        copies[i].wait()
        for left in range(0, wide, step):
            product = jnp.dot(normed[...], up[:, left : left + step], preferred_element_type=f32)
            at = i * wide + left
            hidden[:, at : at + step] = jax.nn.gelu(product).astype(bf16)
    for copy in copies[2:]:
        copy.wait()

    def project(order):
        for j in range(shares):
            at = slice(j * cols, (j + 1) * cols)
            total = jnp.dot(hidden[:, :wide], downs[0][:, at], preferred_element_type=f32)
            total += jnp.dot(hidden[:, wide:], downs[1][:, at], preferred_element_type=f32)
            outs[order[j]][...] = total.astype(bf16)

    in_order(where_ref[0], shares, project)


def expert_project(where, gain, parts, ups, downs):
    rows, cols = parts[0].shape
    shares = len(parts)
    width, wide = ups[0].shape
    return call(
        functools.partial(expert_kernel, shares),
        [jax.ShapeDtypeStruct((rows, cols), bf16)] * shares,
        [SMEM, VMEM] + [VMEM] * shares + [HBM] * 4,
        [VMEM] * shares,
        [
            pltpu.VMEM((rows, width), bf16),
            pltpu.VMEM((rows, 2 * wide), bf16),
            pltpu.VMEM((width, wide), bf16),
            pltpu.VMEM((width, wide), bf16),
            pltpu.VMEM((wide, width), bf16),
            pltpu.VMEM((wide, width), bf16),
            pltpu.SemaphoreType.DMA((4,)),
        ],
        28,
        8 * rows * width * wide,
        8 * width * wide + rows * width * 4,
        where,
        gain,
        *parts,
        *ups,
        *downs,
    )


def sum_kernel(pieces, *refs):
    values, outs = refs[:pieces], refs[pieces:]
    rows = outs[0].shape[0]
    for i, out in enumerate(outs):
        at = slice(i * rows, (i + 1) * rows)
        total = values[0][at].astype(f32)
        for value in values[1:]:
            total = total + value[at].astype(f32)
        out[...] = total.astype(bf16)


def sum_blocks(values, blocks):
    rows, cols = values[0].shape
    return call(
        functools.partial(sum_kernel, len(values)),
        [jax.ShapeDtypeStruct((rows // blocks, cols), bf16)] * blocks,
        [VMEM] * len(values),
        [VMEM] * blocks,
        [],
        8,
        rows * cols * 2,
        rows * cols * 2 * (len(values) + 1),
        *values,
    )


def combine_kernel(firsts, blocks, where_ref, place_ref, base_ref, *refs):
    sources, outs = refs[: len(firsts)], refs[len(firsts) :]
    choices = 2
    for i in range(blocks):
        rows = base_ref.shape[0] // blocks
        at = slice(i * rows, (i + 1) * rows)
        start = pl.multiple_of(where_ref[i] * rows, rows)
        table = place_ref[pl.ds(start, rows)]
        place, gate = table[:, :choices].astype(jnp.int32), table[:, choices : 2 * choices]
        total = base_ref[at].astype(f32)
        for first, source in zip(firsts, sources):
            many = source.shape[0]
            lanes = lax.broadcasted_iota(jnp.int32, (rows, many), 1) + first
            weight = jnp.zeros((rows, many), f32)
            for k in range(choices):
                weight = jnp.where(lanes == place[:, k : k + 1], gate[:, k : k + 1], weight)
            total = total + jnp.dot(weight.astype(bf16), source[...], preferred_element_type=f32)
        if len(outs) == 1:
            outs[0][at] = total
        else:
            outs[i][...] = total.astype(bf16)


def combine(where, places, base, sources, firsts, last):
    blocks = where.shape[0]
    rows, cols = base.shape
    many = sum(source.shape[0] for source in sources)
    shapes = [jax.ShapeDtypeStruct((rows, cols), f32)]
    if last:
        shapes = [jax.ShapeDtypeStruct((rows // blocks, cols), bf16)] * blocks
    return call(
        functools.partial(combine_kernel, firsts, blocks),
        shapes,
        [SMEM, VMEM, VMEM] + [VMEM] * len(sources),
        [VMEM] * len(shapes),
        [],
        20,
        2 * rows * many * cols,
        rows * cols * 6 + many * cols * 2,
        where,
        places,
        base,
        *sources,
    )


def qkv_kernel(shares, where_ref, gain_ref, weight_ref, *refs):
    parts, out, normed, held, sem = refs[:shares], *refs[-4:]
    rows = parts[0].shape[0]
    heads = out.shape[1]

    def norm(order):
        values = jnp.concatenate([parts[d][...].astype(f32) for d in order], 1)
        normed[...] = normalised(values, gain_ref[...])

    in_order(where_ref[0], shares, norm)
    to = pl.ds(pl.multiple_of(where_ref[1] * rows, rows), rows)
    copies = []
    for j in range(out.shape[0]):
        result = lax.dot_general(
            weight_ref[j * heads : (j + 1) * heads],
            normed[...],
            (((1,), (1,)), ((), ())),
            preferred_element_type=f32,
        )
        held[j] = result.astype(bf16)
        copies.append(pltpu.make_async_copy(held.at[j], out.at[j, :, to], sem.at[j]))
        copies[-1].start()
    for copy in copies:
        copy.wait()


def qkv_project(where, gain, weight, parts, total, earlier):
    shares = len(parts)
    rows = parts[0].shape[0]
    wide, width = weight.shape
    inputs = [where, gain, weight, *parts] + ([] if earlier is None else [earlier])
    return pl.pallas_call(
        functools.partial(qkv_kernel, shares),
        out_shape=jax.ShapeDtypeStruct((3, wide // 3, total), bf16),
        in_specs=[SMEM, VMEM, VMEM] + [VMEM] * shares + [HBM] * (earlier is not None),
        out_specs=HBM,
        scratch_shapes=[
            pltpu.VMEM((rows, width), bf16),
            pltpu.VMEM((3, wide // 3, rows), bf16),
            pltpu.SemaphoreType.DMA((3,)),
        ],
        input_output_aliases={} if earlier is None else {3 + shares: 0},
        compiler_params=pltpu.CompilerParams(vmem_limit_bytes=20 << 20),
        cost_estimate=pl.CostEstimate(
            flops=2 * rows * width * wide,
            bytes_accessed=rows * (width + wide) * 2 + width * wide * 2,
            transcendentals=0,
        ),
    )(*inputs)


def local(
    tokens,
    time_taps,
    norm_gain,
    expert_ids,
    priority_ranks,
    keep_mask,
    gate_weights,
    up_weight,
    down_weight,
    attn_gain,
    qkv_weight,
):
    frames_here, patches, width = tokens.shape[1:]
    members = lax.axis_size("tm")
    experts = lax.axis_size("expert")
    chips = members // 2
    cols = width // chips
    place = lax.axis_index("tm")
    chip, core = place // 2, place % 2
    me = lax.axis_index("expert")
    own_rows = frames_here * patches
    rows = own_rows * members
    capacity = rows * expert_ids.shape[2] // (2 * experts)
    half = capacity // 2

    def columns_of(value, d):
        return lax.dynamic_slice_in_dim(value, (chip ^ d) * cols, cols, value.ndim - 1)

    def rows_of(value, i):
        return lax.dynamic_slice_in_dim(value, (2 * i + core) * own_rows, own_rows, 1)

    own_tokens = tokens.reshape(own_rows, width)
    theirs = [columns_of(own_tokens, d) for d in range(1, chips)]
    mine = columns_of(after(own_tokens, *theirs), 0)
    near = [mine] + [swap(value, "tm", 2 * d) for d, value in enumerate(theirs, 1)]
    over = [swap(value, "tm", 1) for value in near]
    token_places = jnp.stack(
        [(chip ^ d) * 2 + core for d in range(chips)]
        + [(chip ^ d) * 2 + 1 - core for d in range(chips)]
    ).astype(jnp.int32)

    ups = [up_weight[0], swap(up_weight[0], "tm", 1)]
    downs = [down_weight[0], swap(down_weight[0], "tm", 1)]
    qkv_columns = jnp.swapaxes(qkv_weight, 1, 2).reshape(-1, width)
    taps = columns_of(time_taps, 0)

    where_chip = chip.astype(jnp.int32)[None]
    blocks_here = jnp.stack([2 * i + core for i in range(chips)]).astype(jnp.int32)
    out_place, back_place = slot_places(
        jnp.stack([me, core]).astype(jnp.int32),
        expert_ids[0].T,
        priority_ranks[0].T,
        keep_mask[0].T,
        gate_weights[0].T,
        half,
        experts,
    )

    near, over, ups, downs, out_place = lax.optimization_barrier(
        (near, over, ups, downs, out_place)
    )
    base, *sent = mix_and_dispatch(
        jnp.concatenate([token_places, blocks_here]),
        taps,
        out_place,
        near + over,
        patches,
        experts,
        half,
    )

    middle = experts // 2
    bounds = [0, middle, middle + middle // 2, experts]
    groups = [range(*pair) for pair in zip(bounds, bounds[1:])]
    arrived = [sent[0]] + [swap(sent[k], "expert", k) for k in range(1, groups[1].stop)]
    last = lax.optimization_barrier(([sent[k] for k in groups[2]], arrived[1:middle]))[0]
    arrived += [swap(value, "expert", k) for k, value in zip(groups[2], last)]
    partial_sums = []
    for group in groups:
        rows_in = jnp.concatenate([arrived[k] for k in group], 0)
        shares = [rows_in] + [swap(rows_in, "tm", 2 * d) for d in range(1, chips)]
        partial_sums.append(expert_project(where_chip, norm_gain[None], shares, ups, downs))

    back = [None] * len(groups)
    first = None
    for g in (1, 2, 0):
        sums = list(partial_sums[g])
        if g == 0:
            sums = after(sums, *first)
        pieces = [sums[0]] + [swap(sums[d], "tm", 2 * d) for d in range(1, chips)]
        first = first or pieces[1:]
        blocks = sum_blocks(pieces, len(groups[g]))
        back[g] = jnp.concatenate(
            [swap(block, "expert", k) if k else block for k, block in zip(groups[g], blocks)], 0
        )
    over_back = [swap(value, "tm", 1) for value in back]
    total = base
    for chosen in ((1, 2), (0,)):
        sources, firsts = [], []
        for g in chosen:
            sources += [back[g], over_back[g]]
            firsts += [groups[g].start * half, (experts + groups[g].start) * half]
        done = combine(blocks_here, back_place, total, sources, firsts, chosen == (0,))
        total = done[0]
    stream = list(done)
    qkv_rows = None
    full = []
    for i in range(chips):
        if i:
            stream[i] = after(stream[i], *full[i - 1])
        pieces = [stream[i]] + [swap(stream[i], "tm", 2 * d) for d in range(1, chips)]
        if i:
            pieces = after(pieces, qkv_rows)
        full.append(pieces)
        other = [swap(piece, "tm", 1) for piece in pieces]
        for side, parts in ((core, pieces), (1 - core, other)):
            where = jnp.stack([chip, 2 * i + side]).astype(jnp.int32)
            qkv_rows = qkv_project(where, attn_gain[None], qkv_columns, parts, rows, qkv_rows)

    stacked = jnp.stack(
        [jnp.where(chip == 0, full[0][d], full[1][d]) for d in range(chips)]
        if chips == 2
        else [jnp.stack([full[i][d] for i in range(chips)])[chip] for d in range(chips)]
    )
    stream_here = jnp.concatenate([stacked[chip ^ i] for i in range(chips)], 1)
    return (stream_here.reshape(tokens.shape), jnp.swapaxes(qkv_rows, 1, 2)[:, None])


def solution(mesh):
    in_specs = (
        P("expert", "tm", None, None),
        P(),
        P(),
        P("expert", None, None),
        P("expert", None, None),
        P("expert", None, None),
        P("expert", None, None),
        P("expert", None, "tm"),
        P("expert", "tm", None),
        P(),
        P(None, None, "tm"),
    )
    out_specs = (P("expert", "tm", None, None), P(None, "expert", None, "tm"))
    return jax.shard_map(local, mesh=mesh, in_specs=in_specs, out_specs=out_specs, check_vma=False)
```

```python
import functools

import jax
import jax.numpy as jnp
from jax import lax
from jax.experimental import pallas as pl
from jax.experimental.pallas import tpu as pltpu
from jax.sharding import PartitionSpec as P

eps = 1e-06
bf16 = jnp.bfloat16
f32 = jnp.float32
HBM = pl.BlockSpec(memory_space=pl.ANY)
VMEM = pl.BlockSpec(memory_space=pltpu.VMEM)
SMEM = pl.BlockSpec(memory_space=pltpu.SMEM)


def call(kernel, out_shape, in_specs, out_specs, scratch, megabytes, flops, moved, *args):
    return pl.pallas_call(
        kernel,
        out_shape=out_shape,
        in_specs=in_specs,
        out_specs=out_specs,
        scratch_shapes=scratch,
        compiler_params=pltpu.CompilerParams(vmem_limit_bytes=megabytes << 20),
        cost_estimate=pl.CostEstimate(flops=3*flops, bytes_accessed=3*moved, transcendentals=0),
    )(*args)


def swap(value, axis, distance):
    count = lax.axis_size(axis)
    return lax.ppermute(value, axis, [(i, i ^ distance) for i in range(count)])


def after(value, *others):
    return lax.optimization_barrier((value, others))[0]


def tile_of(rows, most=512):
    return most if rows % most == 0 else rows


def places_kernel(half, experts, where_ref, ids_ref, ranks_ref, keep_ref, gate_ref, out_ref, back_ref):
    me, core = where_ref[0], where_ref[1]
    ids, ranks, kept = ids_ref[...] ^ me, ranks_ref[...], keep_ref[...] == 1
    own = ranks - core * half
    out_ref[...] = jnp.where(kept & (own >= 0) & (own < half), ids * half + own, -1)
    upper = jnp.where(ranks >= half, 1, 0)
    back = ((upper ^ core) * experts + ids) * half + ranks - upper * half
    table = [jnp.where(kept, back, -1).astype(f32), gate_ref[...]]
    filler = jnp.zeros((8 - 2 * ids.shape[0], ids.shape[1]), f32)
    back_ref[...] = jnp.concatenate(table + [filler], 0).T


def slot_places(where, ids, ranks, keep, gates, half, experts):
    choices, rows = ids.shape
    return call(
        functools.partial(places_kernel, half, experts),
        [
            jax.ShapeDtypeStruct((choices, rows), jnp.int32),
            jax.ShapeDtypeStruct((rows, 8), f32),
        ],
        [SMEM] + [VMEM] * 4,
        [VMEM] * 2,
        [],
        8,
        rows * 64,
        rows * 512,
        where,
        ids,
        ranks,
        keep,
        gates,
    )


def dispatch_kernel(blocks, patches, per, where_ref, taps_ref, place_ref, *refs):
    tokens, refs = refs[:blocks], refs[blocks:]
    base_ref, outs, (extended, mixed_ref, sems) = refs[0], refs[1:-3], refs[-3:]
    rows = tokens[0].shape[0]
    copies = [
        pltpu.make_async_copy(
            tokens[i],
            extended.at[pl.ds(pl.multiple_of(where_ref[i] * rows, rows), rows)],
            sems.at[i],
        )
        for i in range(blocks)
    ]
    for copy in copies:
        copy.start()
    for copy in copies:
        copy.wait()
    frames = blocks * rows // patches
    width = extended.shape[1]
    for left in range(0, width, 128):
        lanes = slice(left, min(left + 128, width))
        taps = [taps_ref[i : i + 1, lanes] for i in range(3)]

        def step(t, carry, lanes=lanes, taps=taps):
            earlier, before = carry
            start = pl.multiple_of(t * patches, patches)
            now = extended[pl.ds(start, patches), lanes].astype(f32)
            mixed = taps[0] * now + taps[1] * before + taps[2] * earlier
            mixed_ref[pl.ds(start, patches), lanes] = mixed.astype(bf16)
            return before, now

        first = extended[0:patches, lanes].astype(f32)
        second = extended[patches : 2 * patches, lanes].astype(f32)
        mixed_ref[0:patches, lanes] = (taps[0] * first).astype(bf16)
        mixed_ref[patches : 2 * patches, lanes] = (taps[0] * second + taps[1] * first).astype(bf16)
        lax.fori_loop(2, frames, step, (first, second), unroll=3)

    place = place_ref[...]
    together = max(1, 512 // per)
    for base in range(0, len(outs), together):
        group = outs[base : base + together]
        size = per * len(group)
        slots = lax.broadcasted_iota(jnp.int32, (size, blocks * rows), 0) + base * per
        hit = (slots == place[0:1]) | (slots == place[1:2])
        picked = jnp.dot(
            jnp.where(hit, 1.0, 0.0).astype(bf16), mixed_ref[...], preferred_element_type=f32
        ).astype(bf16)
        for i, out in enumerate(group):
            out[...] = picked[i * per : (i + 1) * per]
    for i in range(blocks // 2):
        start = pl.multiple_of(where_ref[blocks + i] * rows, rows)
        base_ref[i * rows : (i + 1) * rows] = mixed_ref[pl.ds(start, rows)]


def mix_and_dispatch(where, taps, place, tokens, patches, experts, per):
    blocks = len(tokens)
    rows, cols = tokens[0].shape
    total = blocks * rows
    return call(
        functools.partial(dispatch_kernel, blocks, patches, per),
        [jax.ShapeDtypeStruct((total // 2, cols), bf16)]
        + [jax.ShapeDtypeStruct((per, cols), bf16)] * experts,
        [SMEM, VMEM, VMEM] + [HBM] * blocks,
        [VMEM] * (1 + experts),
        [
            pltpu.VMEM((total, cols), bf16),
            pltpu.VMEM((total, cols), bf16),
            pltpu.SemaphoreType.DMA((blocks,)),
        ],
        24,
        2 * total * per * experts * cols,
        total * cols * 2 + experts * per * cols * 2,
        where,
        taps,
        place,
        *tokens,
    )


def normalised(values, gain):
    scale = 1.0 / values.shape[1]
    center = values - jnp.sum(values, -1, keepdims=True) * scale
    spread = jnp.sum(center * center, -1, keepdims=True) * scale
    return (center * lax.rsqrt(spread + eps) * gain).astype(bf16)


def in_order(chip, shares, run):
    for i in range(shares):

        @pl.when(chip == i)
        def _(i=i):
            run([i ^ j for j in range(shares)])


def expert_kernel(shares, where_ref, gain_ref, *refs):
    parts, refs = refs[:shares], refs[shares:]
    weights, refs = refs[:4], refs[4:]
    outs, refs = refs[:shares], refs[shares:]
    normed, hidden, held, sems = refs[0], refs[1], refs[2:6], refs[6]
    rows, cols = parts[0].shape
    copies = [
        pltpu.make_async_copy(weight, place, sems.at[i])
        for i, (weight, place) in enumerate(zip(weights, held))
    ]
    ups, downs = held[:2], held[2:]
    wide = ups[0].shape[1]
    step = 256 if wide % 256 == 0 else wide
    for copy in copies:
        copy.start()

    def run(order):
        values = jnp.concatenate([parts[d][...].astype(f32) for d in order], 1)
        normed[...] = normalised(values, gain_ref[...])
        for i, up in enumerate(ups):
            copies[i].wait()
            for left in range(0, wide, step):
                product = jnp.dot(
                    normed[...], up[:, left : left + step], preferred_element_type=f32
                )
                at = i * wide + left
                hidden[:, at : at + step] = jax.nn.gelu(product).astype(bf16)
        copies[2].wait()
        copies[3].wait()
        for j in range(shares):
            at = slice(j * cols, (j + 1) * cols)
            total = jnp.dot(hidden[:, :wide], downs[0][:, at], preferred_element_type=f32)
            total += jnp.dot(hidden[:, wide:], downs[1][:, at], preferred_element_type=f32)
            outs[order[j]][...] = total.astype(bf16)

    in_order(where_ref[0], shares, run)


def expert_project(where, gain, parts, weights):
    rows, cols = parts[0].shape
    shares = len(parts)
    width, wide = weights[0].shape
    return call(
        functools.partial(expert_kernel, shares),
        [jax.ShapeDtypeStruct((rows, cols), bf16)] * shares,
        [SMEM, VMEM] + [VMEM] * shares + [HBM] * 4,
        [VMEM] * shares,
        [
            pltpu.VMEM((rows, width), bf16),
            pltpu.VMEM((rows, 2 * wide), bf16),
            pltpu.VMEM((width, wide), bf16),
            pltpu.VMEM((width, wide), bf16),
            pltpu.VMEM((wide, width), bf16),
            pltpu.VMEM((wide, width), bf16),
            pltpu.SemaphoreType.DMA((4,)),
        ],
        24,
        8 * rows * width * wide,
        8 * width * wide + rows * width * 4,
        where,
        gain,
        *parts,
        *weights,
    )


def sum_kernel(pieces, *refs):
    values, outs = refs[:pieces], refs[pieces:]
    rows = outs[0].shape[0]
    for i, out in enumerate(outs):
        at = slice(i * rows, (i + 1) * rows)
        total = values[0][at].astype(f32)
        for value in values[1:]:
            total = total + value[at].astype(f32)
        out[...] = total.astype(bf16)


def sum_blocks(values, blocks):
    rows, cols = values[0].shape
    return call(
        functools.partial(sum_kernel, len(values)),
        [jax.ShapeDtypeStruct((rows // blocks, cols), bf16)] * blocks,
        [VMEM] * len(values),
        [VMEM] * blocks,
        [],
        8,
        rows * cols * 2,
        rows * cols * 2 * (len(values) + 1),
        *values,
    )


def combine_kernel(firsts, blocks, where_ref, place_ref, base_ref, *refs):
    sources, outs = refs[: len(firsts)], refs[len(firsts) :]
    choices = 2
    for i in range(blocks):
        rows = base_ref.shape[0] // blocks
        at = slice(i * rows, (i + 1) * rows)
        start = pl.multiple_of(where_ref[i] * rows, rows)
        table = place_ref[pl.ds(start, rows)]
        place, gate = table[:, :choices].astype(jnp.int32), table[:, choices : 2 * choices]
        total = base_ref[at].astype(f32)
        for first, source in zip(firsts, sources):
            many = source.shape[0]
            lanes = lax.broadcasted_iota(jnp.int32, (rows, many), 1) + first
            weight = jnp.zeros((rows, many), f32)
            for k in range(choices):
                weight = jnp.where(lanes == place[:, k : k + 1], gate[:, k : k + 1], weight)
            total = total + jnp.dot(weight.astype(bf16), source[...], preferred_element_type=f32)
        if len(outs) == 1:
            outs[0][at] = total
        else:
            outs[i][...] = total.astype(bf16)


def combine(where, places, base, sources, firsts, last):
    blocks = where.shape[0]
    rows, cols = base.shape
    many = sum(source.shape[0] for source in sources)
    shapes = [jax.ShapeDtypeStruct((rows, cols), f32)]
    if last:
        shapes = [jax.ShapeDtypeStruct((rows // blocks, cols), bf16)] * blocks
    return call(
        functools.partial(combine_kernel, firsts, blocks),
        shapes,
        [SMEM, VMEM, VMEM] + [VMEM] * len(sources),
        [VMEM] * len(shapes),
        [],
        20,
        2 * rows * many * cols,
        rows * cols * 6 + many * cols * 2,
        where,
        places,
        base,
        *sources,
    )


def qkv_kernel(shares, block, earlier, where_ref, gain_ref, weight_ref, *refs):
    parts, refs = refs[:shares], refs[shares + earlier :]
    out, refs = refs[0], refs[1:]
    if block is not None:
        stream, stage, stage_sem, refs = refs[0], refs[-2], refs[-1], refs[1:-2]
    normed, held, weights, sem, weight_sem = refs
    rows = parts[0].shape[0]
    heads = out.shape[1]
    loads = []
    for j in range(3):
        at = slice(j * heads, (j + 1) * heads)
        loads.append(
            pltpu.make_async_copy(weight_ref.at[at], weights.at[at], weight_sem.at[j])
        )
        loads[-1].start()

    to = pl.ds(pl.multiple_of(where_ref[1] * rows, rows), rows)
    copies = [pltpu.make_async_copy(held.at[j], out.at[j, :, to], sem.at[j]) for j in range(3)]
    tile = tile_of(rows, 256)

    def run(order):
        if block is not None and order[block] == 0:
            stage[...] = jnp.concatenate([parts[d][...] for d in order], 1)
            pltpu.make_async_copy(stage, stream, stage_sem).start()
        for left in range(0, rows, tile):
            at = slice(left, left + tile)
            values = jnp.concatenate([parts[d][at].astype(f32) for d in order], 1)
            normed[at] = normalised(values, gain_ref[...])
        for j, copy in enumerate(copies):
            loads[j].wait()
            for left in range(0, rows, tile):
                at = slice(left, left + tile)
                result = lax.dot_general(
                    weights[j * heads : (j + 1) * heads],
                    normed[at],
                    (((1,), (1,)), ((), ())),
                    preferred_element_type=f32,
                )
                held[j, :, at] = result.astype(bf16)
            copy.start()

    in_order(where_ref[0], shares, run)
    for copy in copies:
        copy.wait()
    if block is not None:

        @pl.when(where_ref[0] == block)
        def _():
            pltpu.make_async_copy(stage, stream, stage_sem).wait()


def qkv_project(where, gain, weight, parts, total, block, earlier):
    shares = len(parts)
    rows = parts[0].shape[0]
    wide, width = weight.shape
    shapes = [jax.ShapeDtypeStruct((3, wide // 3, total), bf16)]
    scratch = [
        pltpu.VMEM((rows, width), bf16),
        pltpu.VMEM((3, wide // 3, rows), bf16),
        pltpu.VMEM((wide, width), bf16),
        pltpu.SemaphoreType.DMA((3,)),
        pltpu.SemaphoreType.DMA((3,)),
    ]
    if block is not None:
        shapes += [jax.ShapeDtypeStruct((rows, width), bf16)]
        scratch += [pltpu.VMEM((rows, width), bf16), pltpu.SemaphoreType.DMA]
    return pl.pallas_call(
        functools.partial(qkv_kernel, shares, block, len(earlier)),
        out_shape=shapes,
        in_specs=[SMEM, VMEM, pl.BlockSpec(memory_space=pltpu.HBM)]
        + [VMEM] * shares
        + [HBM] * len(earlier),
        out_specs=[HBM] * len(shapes),
        scratch_shapes=scratch,
        input_output_aliases={3 + shares + i: i for i in range(len(earlier))},
        compiler_params=pltpu.CompilerParams(vmem_limit_bytes=20 << 20),
        cost_estimate=pl.CostEstimate(
            flops=2 * rows * width * wide,
            bytes_accessed=rows * (width + wide) * 2 + width * wide * 2,
            transcendentals=0,
        ),
    )(where, gain, weight, *parts, *earlier)


def local(
    tokens,
    time_taps,
    norm_gain,
    expert_ids,
    priority_ranks,
    keep_mask,
    gate_weights,
    up_weight,
    down_weight,
    attn_gain,
    qkv_weight,
):
    frames_here, patches, width = tokens.shape[1:]
    members = lax.axis_size("tm")
    experts = lax.axis_size("expert")
    chips = members // 2
    cols = width // chips
    place = lax.axis_index("tm")
    chip, core = place // 2, place % 2
    me = lax.axis_index("expert")
    own_rows = frames_here * patches
    rows = own_rows * members
    capacity = rows * expert_ids.shape[2] // (2 * experts)
    half = capacity // 2

    def columns_of(value, d):
        return lax.dynamic_slice_in_dim(value, (chip ^ d) * cols, cols, value.ndim - 1)

    def rows_of(value, i):
        return lax.dynamic_slice_in_dim(value, (2 * i + core) * own_rows, own_rows, 1)

    own_tokens = tokens.reshape(own_rows, width)
    theirs = [columns_of(own_tokens, d) for d in range(1, chips)]
    mine = columns_of(after(own_tokens, *theirs), 0)
    near = [mine] + [swap(value, "tm", 2 * d) for d, value in enumerate(theirs, 1)]
    over = [swap(value, "tm", 1) for value in near]
    token_places = jnp.stack(
        [(chip ^ d) * 2 + core for d in range(chips)]
        + [(chip ^ d) * 2 + 1 - core for d in range(chips)]
    ).astype(jnp.int32)

    ups = [up_weight[0], swap(up_weight[0], "tm", 1)]
    downs = [down_weight[0], swap(down_weight[0], "tm", 1)]
    qkv_columns = pltpu.with_memory_space_constraint(
        jnp.swapaxes(qkv_weight, 1, 2).reshape(-1, width), pltpu.HBM
    )
    taps = columns_of(time_taps, 0)

    where_chip = chip.astype(jnp.int32)[None]
    blocks_here = jnp.stack([2 * i + core for i in range(chips)]).astype(jnp.int32)
    out_place, back_place = slot_places(
        jnp.stack([me, core]).astype(jnp.int32),
        expert_ids[0].T,
        priority_ranks[0].T,
        keep_mask[0].T,
        gate_weights[0].T,
        half,
        experts,
    )

    weights = ups + downs
    near, over, weights, out_place = lax.optimization_barrier((near, over, weights, out_place))
    base, *sent = mix_and_dispatch(
        jnp.concatenate([token_places, blocks_here]),
        taps,
        out_place,
        near + over,
        patches,
        experts,
        half,
    )

    middle = experts // 2
    bounds = [0, middle // 2, middle, middle + middle // 2, experts]
    groups = [range(*pair) for pair in zip(bounds, bounds[1:])]
    arrived = [sent[0]] + [swap(sent[k], "expert", k) for k in range(1, groups[2].stop)]
    partial_sums = []
    for group in groups:
        rows_in = jnp.concatenate([arrived[k] for k in group], 0)
        shares = [rows_in] + [swap(rows_in, "tm", 2 * d) for d in range(1, chips)]
        if not partial_sums:
            last = after([sent[k] for k in groups[3]], *shares[1:])
            arrived += [swap(value, "expert", k) for k, value in zip(groups[3], last)]
        else:
            shares = after(shares, *partial_sums[-1])
        partial_sums.append(expert_project(where_chip, norm_gain[None], shares, weights))

    returned = [None] * len(groups)
    received = {}
    for g, follows in ((2, None), (3, None), (1, 2), (0, 3)):
        sums = list(partial_sums[g])
        if follows:
            sums = after(sums, *received[follows])
        received[g] = [swap(sums[d], "tm", 2 * d) for d in range(1, chips)]
        blocks = sum_blocks([sums[0]] + received[g], len(groups[g]))
        returned[g] = [
            swap(block, "expert", k) if k else block for k, block in zip(groups[g], blocks)
        ]
    returned = after(returned, *received[0], *received[1])
    back = [jnp.concatenate(blocks, 0) for blocks in returned]
    over_back = [swap(value, "tm", 1) for value in back]
    total = base
    steps = [[(2, 0), (2, 1)], [(0, 0), (1, 0), (3, 0)], [(0, 1), (1, 1), (3, 1)]]
    for step in steps:
        sources = [(over_back if side else back)[g] for g, side in step]
        firsts = [(side * experts + groups[g].start) * half for g, side in step]
        done = combine(blocks_here, back_place, total, sources, firsts, step is steps[-1])
        total = done[0]
    stream = list(done)
    qkv_rows, own_stream, before = [], [], None
    for i in range(chips):
        if before:
            stream[i] = after(stream[i], *before)
        pieces = [stream[i]] + [swap(stream[i], "tm", 2 * d) for d in range(1, chips)]
        before = pieces
        if i:
            pieces = after(pieces, *qkv_rows)
        other = [swap(piece, "tm", 1) for piece in pieces]
        where = jnp.stack([chip, 2 * i + core]).astype(jnp.int32)
        *qkv_rows, own = qkv_project(
            where, attn_gain[None], qkv_columns, pieces, rows, i, qkv_rows + own_stream
        )
        own_stream = [own]
        where = jnp.stack([chip, 2 * i + 1 - core]).astype(jnp.int32)
        qkv_rows = list(
            qkv_project(where, attn_gain[None], qkv_columns, other, rows, None, qkv_rows)
        )
    return (own_stream[0].reshape(tokens.shape), jnp.swapaxes(qkv_rows[0], 1, 2)[:, None])


def solution(mesh):
    in_specs = (
        P("expert", "tm", None, None),
        P(),
        P(),
        P("expert", None, None),
        P("expert", None, None),
        P("expert", None, None),
        P("expert", None, None),
        P("expert", None, "tm"),
        P("expert", "tm", None),
        P(),
        P(None, None, "tm"),
    )
    out_specs = (P("expert", "tm", None, None), P(None, "expert", None, "tm"))
    return jax.shard_map(local, mesh=mesh, in_specs=in_specs, out_specs=out_specs, check_vma=False)
```

```python
import functools

import jax
import jax.numpy as jnp
from jax import lax
from jax.experimental import pallas as pl
from jax.experimental.pallas import tpu as pltpu
from jax.sharding import PartitionSpec as P

eps = 1e-06
bf16 = jnp.bfloat16
f32 = jnp.float32
HBM = pl.BlockSpec(memory_space=pl.ANY)
VMEM = pl.BlockSpec(memory_space=pltpu.VMEM)
SMEM = pl.BlockSpec(memory_space=pltpu.SMEM)


def call(kernel, out_shape, in_specs, out_specs, scratch, megabytes, flops, moved, *args):
    return pl.pallas_call(
        kernel,
        out_shape=out_shape,
        in_specs=in_specs,
        out_specs=out_specs,
        scratch_shapes=scratch,
        compiler_params=pltpu.CompilerParams(vmem_limit_bytes=megabytes << 20),
        cost_estimate=pl.CostEstimate(flops=3*flops, bytes_accessed=3*moved, transcendentals=0),
    )(*args)


def swap(value, axis, distance):
    count = lax.axis_size(axis)
    return lax.ppermute(value, axis, [(i, i ^ distance) for i in range(count)])


def after(value, *others):
    return lax.optimization_barrier((value, others))[0]


def tile_of(rows, most=512):
    return most if rows % most == 0 else rows


def places_kernel(half, experts, where_ref, ids_ref, ranks_ref, keep_ref, gate_ref, out_ref, back_ref):
    me, core = where_ref[0], where_ref[1]
    ids, ranks, kept = ids_ref[...] ^ me, ranks_ref[...], keep_ref[...] == 1
    own = ranks - core * half
    out_ref[...] = jnp.where(kept & (own >= 0) & (own < half), ids * half + own, -1)
    upper = jnp.where(ranks >= half, 1, 0)
    back = ((upper ^ core) * experts + ids) * half + ranks - upper * half
    table = [jnp.where(kept, back, -1).astype(f32), gate_ref[...]]
    filler = jnp.zeros((8 - 2 * ids.shape[0], ids.shape[1]), f32)
    back_ref[...] = jnp.concatenate(table + [filler], 0).T


def slot_places(where, ids, ranks, keep, gates, half, experts):
    choices, rows = ids.shape
    return call(
        functools.partial(places_kernel, half, experts),
        [
            jax.ShapeDtypeStruct((choices, rows), jnp.int32),
            jax.ShapeDtypeStruct((rows, 8), f32),
        ],
        [SMEM] + [VMEM] * 4,
        [VMEM] * 2,
        [],
        8,
        rows * 64,
        rows * 512,
        where,
        ids,
        ranks,
        keep,
        gates,
    )


def dispatch_kernel(blocks, patches, per, where_ref, taps_ref, place_ref, *refs):
    tokens, refs = refs[:blocks], refs[blocks:]
    base_ref, outs, (extended, mixed_ref, sems) = refs[0], refs[1:-3], refs[-3:]
    rows = tokens[0].shape[0]
    copies = [
        pltpu.make_async_copy(
            tokens[i],
            extended.at[pl.ds(pl.multiple_of(where_ref[i] * rows, rows), rows)],
            sems.at[i],
        )
        for i in range(blocks)
    ]
    for copy in copies:
        copy.start()
    for copy in copies:
        copy.wait()
    frames = blocks * rows // patches
    width = extended.shape[1]
    for left in range(0, width, 128):
        lanes = slice(left, min(left + 128, width))
        taps = [taps_ref[i : i + 1, lanes] for i in range(3)]

        def step(t, carry, lanes=lanes, taps=taps):
            earlier, before = carry
            start = pl.multiple_of(t * patches, patches)
            now = extended[pl.ds(start, patches), lanes].astype(f32)
            mixed = taps[0] * now + taps[1] * before + taps[2] * earlier
            mixed_ref[pl.ds(start, patches), lanes] = mixed.astype(bf16)
            return before, now

        first = extended[0:patches, lanes].astype(f32)
        second = extended[patches : 2 * patches, lanes].astype(f32)
        mixed_ref[0:patches, lanes] = (taps[0] * first).astype(bf16)
        mixed_ref[patches : 2 * patches, lanes] = (taps[0] * second + taps[1] * first).astype(bf16)
        lax.fori_loop(2, frames, step, (first, second), unroll=3)

    place = place_ref[...]
    together = max(1, 512 // per)
    for base in range(0, len(outs), together):
        group = outs[base : base + together]
        size = per * len(group)
        slots = lax.broadcasted_iota(jnp.int32, (size, blocks * rows), 0) + base * per
        hit = (slots == place[0:1]) | (slots == place[1:2])
        picked = jnp.dot(
            jnp.where(hit, 1.0, 0.0).astype(bf16), mixed_ref[...], preferred_element_type=f32
        ).astype(bf16)
        for i, out in enumerate(group):
            out[...] = picked[i * per : (i + 1) * per]
    for i in range(blocks // 2):
        start = pl.multiple_of(where_ref[blocks + i] * rows, rows)
        base_ref[i * rows : (i + 1) * rows] = mixed_ref[pl.ds(start, rows)]


def mix_and_dispatch(where, taps, place, tokens, patches, experts, per):
    blocks = len(tokens)
    rows, cols = tokens[0].shape
    total = blocks * rows
    return call(
        functools.partial(dispatch_kernel, blocks, patches, per),
        [jax.ShapeDtypeStruct((total // 2, cols), bf16)]
        + [jax.ShapeDtypeStruct((per, cols), bf16)] * experts,
        [SMEM, VMEM, VMEM] + [HBM] * blocks,
        [VMEM] * (1 + experts),
        [
            pltpu.VMEM((total, cols), bf16),
            pltpu.VMEM((total, cols), bf16),
            pltpu.SemaphoreType.DMA((blocks,)),
        ],
        24,
        2 * total * per * experts * cols,
        total * cols * 2 + experts * per * cols * 2,
        where,
        taps,
        place,
        *tokens,
    )


def normalise(parts, starts, gain_ref, out):
    cols = parts[0].shape[1]
    scale = 1.0 / gain_ref.shape[1]
    values = [part.astype(f32) for part in parts]
    mean = sum(jnp.sum(value, -1, keepdims=True) for value in values) * scale
    values = [value - mean for value in values]
    spread = sum(jnp.sum(value * value, -1, keepdims=True) for value in values) * scale
    factor = lax.rsqrt(spread + eps)
    for value, start in zip(values, starts):
        at = pl.ds(start, cols)
        out[:, at] = (value * factor * gain_ref[:, at]).astype(bf16)


def in_place(chip, shares, cols, run):
    if cols % 128 == 0:
        run([pl.multiple_of((chip ^ d) * cols, 128) for d in range(shares)])
        return
    for i in range(shares):

        @pl.when(chip == i)
        def _(i=i):
            run([(i ^ d) * cols for d in range(shares)])


def expert_kernel(shares, where_ref, gain_ref, *refs):
    parts, refs = refs[:shares], refs[shares:]
    weights, refs = refs[:4], refs[4:]
    outs, refs = refs[:shares], refs[shares:]
    normed, hidden, held, sems = refs[0], refs[1], refs[2:6], refs[6]
    rows, cols = parts[0].shape
    copies = [
        pltpu.make_async_copy(weight, place, sems.at[i])
        for i, (weight, place) in enumerate(zip(weights, held))
    ]
    ups, downs = held[:2], held[2:]
    wide = ups[0].shape[1]
    step = 256 if wide % 256 == 0 else wide
    for copy in copies:
        copy.start()

    def run(starts):
        normalise([part[...] for part in parts], starts, gain_ref, normed)
        for i, up in enumerate(ups):
            copies[i].wait()
            for left in range(0, wide, step):
                product = jnp.dot(
                    normed[...], up[:, left : left + step], preferred_element_type=f32
                )
                at = i * wide + left
                hidden[:, at : at + step] = jax.nn.gelu(product).astype(bf16)
        copies[2].wait()
        copies[3].wait()
        for out, start in zip(outs, starts):
            at = pl.ds(start, cols)
            total = jnp.dot(hidden[:, :wide], downs[0][:, at], preferred_element_type=f32)
            total += jnp.dot(hidden[:, wide:], downs[1][:, at], preferred_element_type=f32)
            out[...] = total.astype(bf16)

    in_place(where_ref[0], shares, cols, run)


def expert_project(where, gain, parts, weights):
    rows, cols = parts[0].shape
    shares = len(parts)
    width, wide = weights[0].shape
    return call(
        functools.partial(expert_kernel, shares),
        [jax.ShapeDtypeStruct((rows, cols), bf16)] * shares,
        [SMEM, VMEM] + [VMEM] * shares + [HBM] * 4,
        [VMEM] * shares,
        [
            pltpu.VMEM((rows, width), bf16),
            pltpu.VMEM((rows, 2 * wide), bf16),
            pltpu.VMEM((width, wide), bf16),
            pltpu.VMEM((width, wide), bf16),
            pltpu.VMEM((wide, width), bf16),
            pltpu.VMEM((wide, width), bf16),
            pltpu.SemaphoreType.DMA((4,)),
        ],
        24,
        8 * rows * width * wide,
        8 * width * wide + rows * width * 4,
        where,
        gain,
        *parts,
        *weights,
    )


def sum_kernel(pieces, *refs):
    values, outs = refs[:pieces], refs[pieces:]
    rows = outs[0].shape[0]
    for i, out in enumerate(outs):
        at = slice(i * rows, (i + 1) * rows)
        total = values[0][at].astype(f32)
        for value in values[1:]:
            total = total + value[at].astype(f32)
        out[...] = total.astype(bf16)


def sum_blocks(values, blocks):
    rows, cols = values[0].shape
    return call(
        functools.partial(sum_kernel, len(values)),
        [jax.ShapeDtypeStruct((rows // blocks, cols), bf16)] * blocks,
        [VMEM] * len(values),
        [VMEM] * blocks,
        [],
        8,
        rows * cols * 2,
        rows * cols * 2 * (len(values) + 1),
        *values,
    )


def combine_kernel(firsts, blocks, where_ref, place_ref, base_ref, *refs):
    sources, outs = refs[: len(firsts)], refs[len(firsts) :]
    choices = 2
    rows = base_ref.shape[0] // blocks

    def add(i):
        at = pl.ds(i * rows if isinstance(i, int) else pl.multiple_of(i * rows, rows), rows)
        start = pl.multiple_of(where_ref[i] * rows, rows)
        table = place_ref[pl.ds(start, rows)]
        place, gate = table[:, :choices].astype(jnp.int32), table[:, choices : 2 * choices]
        total = base_ref[at].astype(f32)
        for first, source in zip(firsts, sources):
            many = source.shape[0]
            lanes = lax.broadcasted_iota(jnp.int32, (rows, many), 1) + first
            weight = jnp.zeros((rows, many), f32)
            for k in range(choices):
                weight = jnp.where(lanes == place[:, k : k + 1], gate[:, k : k + 1], weight)
            total = total + jnp.dot(weight.astype(bf16), source[...], preferred_element_type=f32)
        if len(outs) == 1:
            outs[0][at] = total
        else:
            outs[i][...] = total.astype(bf16)

    if len(outs) == 1:
        lax.fori_loop(0, blocks, lambda i, carry: (add(i), carry)[1], 0)
    else:
        for i in range(blocks):
            add(i)


def combine(where, places, base, sources, firsts, last):
    blocks = where.shape[0]
    rows, cols = base.shape
    many = sum(source.shape[0] for source in sources)
    shapes = [jax.ShapeDtypeStruct((rows, cols), f32)]
    if last:
        shapes = [jax.ShapeDtypeStruct((rows // blocks, cols), bf16)] * blocks
    return call(
        functools.partial(combine_kernel, firsts, blocks),
        shapes,
        [SMEM, VMEM, VMEM] + [VMEM] * len(sources),
        [VMEM] * len(shapes),
        [],
        20,
        2 * rows * many * cols,
        rows * cols * 6 + many * cols * 2,
        where,
        places,
        base,
        *sources,
    )


def qkv_kernel(shares, block, earlier, where_ref, gain_ref, weight_ref, *refs):
    parts, refs = refs[:shares], refs[shares + earlier :]
    out, refs = refs[0], refs[1:]
    if block is not None:
        stream, stage, stage_sem, refs = refs[0], refs[-2], refs[-1], refs[1:-2]
    normed, held, weights, sem, weight_sem = refs
    rows, cols = parts[0].shape
    heads = out.shape[1]
    loads = []
    for j in range(3):
        at = slice(j * heads, (j + 1) * heads)
        loads.append(
            pltpu.make_async_copy(weight_ref.at[at], weights.at[at], weight_sem.at[j])
        )
        loads[-1].start()

    to = pl.ds(pl.multiple_of(where_ref[1] * rows, rows), rows)
    copies = [
        pltpu.make_async_copy(
            held.at[j * heads : (j + 1) * heads], out.at[j, :, to], sem.at[j]
        )
        for j in range(3)
    ]
    tile = tile_of(rows, 256)

    def run(starts):
        if block is not None:
            @pl.when(where_ref[0] == block)
            def _():
                for part, start in zip(parts, starts):
                    stage[:, pl.ds(start, cols)] = part[...]
                pltpu.make_async_copy(stage, stream, stage_sem).start()

        for left in range(0, rows, tile):
            at = slice(left, left + tile)
            normalise([part[at] for part in parts], starts, gain_ref, normed.at[at])
        for load in loads:
            load.wait()
        for left in range(0, rows, tile):
            at = slice(left, left + tile)
            result = lax.dot_general(
                weights[...], normed[at], (((1,), (1,)), ((), ())), preferred_element_type=f32
            )
            held[:, at] = result.astype(bf16)
        for copy in copies:
            copy.start()

    in_place(where_ref[0], shares, cols, run)
    for copy in copies:
        copy.wait()
    if block is not None:

        @pl.when(where_ref[0] == block)
        def _():
            pltpu.make_async_copy(stage, stream, stage_sem).wait()


def qkv_project(where, gain, weight, parts, total, block, earlier):
    shares = len(parts)
    rows = parts[0].shape[0]
    wide, width = weight.shape
    shapes = [jax.ShapeDtypeStruct((3, wide // 3, total), bf16)]
    scratch = [
        pltpu.VMEM((rows, width), bf16),
        pltpu.VMEM((wide, rows), bf16),
        pltpu.VMEM((wide, width), bf16),
        pltpu.SemaphoreType.DMA((3,)),
        pltpu.SemaphoreType.DMA((3,)),
    ]
    if block is not None:
        shapes += [jax.ShapeDtypeStruct((rows, width), bf16)]
        scratch += [pltpu.VMEM((rows, width), bf16), pltpu.SemaphoreType.DMA]
    return pl.pallas_call(
        functools.partial(qkv_kernel, shares, block, len(earlier)),
        out_shape=shapes,
        in_specs=[SMEM, VMEM, pl.BlockSpec(memory_space=pltpu.HBM)]
        + [VMEM] * shares
        + [HBM] * len(earlier),
        out_specs=[HBM] * len(shapes),
        scratch_shapes=scratch,
        input_output_aliases={3 + shares + i: i for i in range(len(earlier))},
        compiler_params=pltpu.CompilerParams(vmem_limit_bytes=20 << 20),
        cost_estimate=pl.CostEstimate(
            flops=2 * rows * width * wide,
            bytes_accessed=rows * (width + wide) * 2 + width * wide * 2,
            transcendentals=0,
        ),
    )(where, gain, weight, *parts, *earlier)


def local(
    tokens,
    time_taps,
    norm_gain,
    expert_ids,
    priority_ranks,
    keep_mask,
    gate_weights,
    up_weight,
    down_weight,
    attn_gain,
    qkv_weight,
):
    frames_here, patches, width = tokens.shape[1:]
    members = lax.axis_size("tm")
    experts = lax.axis_size("expert")
    chips = members // 2
    cols = width // chips
    place = lax.axis_index("tm")
    chip, core = place // 2, place % 2
    me = lax.axis_index("expert")
    own_rows = frames_here * patches
    rows = own_rows * members
    capacity = rows * expert_ids.shape[2] // (2 * experts)
    half = capacity // 2

    def columns_of(value, d):
        return lax.dynamic_slice_in_dim(value, (chip ^ d) * cols, cols, value.ndim - 1)

    def rows_of(value, i):
        return lax.dynamic_slice_in_dim(value, (2 * i + core) * own_rows, own_rows, 1)

    own_tokens = tokens.reshape(own_rows, width)
    theirs = [columns_of(own_tokens, d) for d in range(1, chips)]
    mine = columns_of(after(own_tokens, *theirs), 0)
    near = [mine] + [swap(value, "tm", 2 * d) for d, value in enumerate(theirs, 1)]
    over = [swap(value, "tm", 1) for value in near]
    token_places = jnp.stack(
        [(chip ^ d) * 2 + core for d in range(chips)]
        + [(chip ^ d) * 2 + 1 - core for d in range(chips)]
    ).astype(jnp.int32)

    ups = [up_weight[0], swap(up_weight[0], "tm", 1)]
    downs = [down_weight[0], swap(down_weight[0], "tm", 1)]
    qkv_columns = pltpu.with_memory_space_constraint(
        jnp.swapaxes(qkv_weight, 1, 2).reshape(-1, width), pltpu.HBM
    )
    taps = columns_of(time_taps, 0)

    where_chip = chip.astype(jnp.int32)[None]
    blocks_here = jnp.stack([2 * i + core for i in range(chips)]).astype(jnp.int32)
    out_place, back_place = slot_places(
        jnp.stack([me, core]).astype(jnp.int32),
        expert_ids[0].T,
        priority_ranks[0].T,
        keep_mask[0].T,
        gate_weights[0].T,
        half,
        experts,
    )

    weights = ups + downs
    near, over, weights, out_place = lax.optimization_barrier((near, over, weights, out_place))
    base, *sent = mix_and_dispatch(
        jnp.concatenate([token_places, blocks_here]),
        taps,
        out_place,
        near + over,
        patches,
        experts,
        half,
    )

    middle = experts // 2
    bounds = [0, middle // 2, middle, middle + middle // 2, experts]
    groups = [range(*pair) for pair in zip(bounds, bounds[1:])]
    arrived = [sent[0]] + [swap(sent[k], "expert", k) for k in range(1, groups[2].stop)]
    partial_sums = []
    for group in groups:
        rows_in = jnp.concatenate([arrived[k] for k in group], 0)
        shares = [rows_in] + [swap(rows_in, "tm", 2 * d) for d in range(1, chips)]
        if not partial_sums:
            last = after([sent[k] for k in groups[3]], *shares[1:])
            arrived += [swap(value, "expert", k) for k, value in zip(groups[3], last)]
        else:
            shares = after(shares, *partial_sums[-1])
        partial_sums.append(expert_project(where_chip, norm_gain[None], shares, weights))

    returned = [None] * len(groups)
    received = [None] * len(groups)
    sent_back = [None] * len(groups)
    for g, follows in ((2, None), (3, None), (1, 2), (0, 3)):
        sums = list(partial_sums[g])
        if follows:
            sums = after(sums, *sent_back[follows])
        received[g] = [swap(sums[d], "tm", 2 * d) for d in range(1, chips)]
        sent_back[g] = sum_blocks([sums[0]] + received[g], len(groups[g]))
        returned[g] = [
            swap(block, "expert", k) if k else block for k, block in zip(groups[g], sent_back[g])
        ]
    for g in (1, 2, 3):
        returned[g] = after(returned[g], *received[0])
    back = [jnp.concatenate(blocks, 0) for blocks in returned]
    over_back = [swap(value, "tm", 1) for value in back]
    total = base
    steps = [[(2, 0), (2, 1)], [(0, 0), (1, 0), (3, 0)], [(0, 1), (1, 1), (3, 1)]]
    for step in steps:
        sources = [(over_back if side else back)[g] for g, side in step]
        firsts = [(side * experts + groups[g].start) * half for g, side in step]
        done = combine(blocks_here, back_place, total, sources, firsts, step is steps[-1])
        total = done[0]
    stream = list(done)
    qkv_rows, own_stream, before = [], [], None
    for i in range(chips):
        if before:
            stream[i] = after(stream[i], *before)
        pieces = [stream[i]] + [swap(stream[i], "tm", 2 * d) for d in range(1, chips)]
        before = pieces
        if i:
            pieces = after(pieces, *qkv_rows)
        other = [swap(piece, "tm", 1) for piece in pieces]
        where = jnp.stack([chip, 2 * i + core]).astype(jnp.int32)
        *qkv_rows, own = qkv_project(
            where, attn_gain[None], qkv_columns, pieces, rows, i, qkv_rows + own_stream
        )
        own_stream = [own]
        where = jnp.stack([chip, 2 * i + 1 - core]).astype(jnp.int32)
        qkv_rows = list(
            qkv_project(where, attn_gain[None], qkv_columns, other, rows, None, qkv_rows)
        )
    return (own_stream[0].reshape(tokens.shape), jnp.swapaxes(qkv_rows[0], 1, 2)[:, None])


def solution(mesh):
    in_specs = (
        P("expert", "tm", None, None),
        P(),
        P(),
        P("expert", None, None),
        P("expert", None, None),
        P("expert", None, None),
        P("expert", None, None),
        P("expert", None, "tm"),
        P("expert", "tm", None),
        P(),
        P(None, None, "tm"),
    )
    out_specs = (P("expert", "tm", None, None), P(None, "expert", None, "tm"))
    return jax.shard_map(local, mesh=mesh, in_specs=in_specs, out_specs=out_specs, check_vma=False)
```

```python
import functools

import jax
import jax.numpy as jnp
from jax import lax
from jax.experimental import pallas as pl
from jax.experimental.pallas import tpu as pltpu
from jax.sharding import PartitionSpec as P

eps = 1e-06
bf16 = jnp.bfloat16
f32 = jnp.float32
HBM = pl.BlockSpec(memory_space=pl.ANY)
VMEM = pl.BlockSpec(memory_space=pltpu.VMEM)
SMEM = pl.BlockSpec(memory_space=pltpu.SMEM)


def call(kernel, out_shape, in_specs, out_specs, scratch, megabytes, flops, moved, *args):
    return pl.pallas_call(
        kernel,
        out_shape=out_shape,
        in_specs=in_specs,
        out_specs=out_specs,
        scratch_shapes=scratch,
        compiler_params=pltpu.CompilerParams(vmem_limit_bytes=megabytes << 20),
        cost_estimate=pl.CostEstimate(flops=3*flops, bytes_accessed=3*moved, transcendentals=0),
    )(*args)


def swap(value, axis, distance):
    count = lax.axis_size(axis)
    return lax.ppermute(value, axis, [(i, i ^ distance) for i in range(count)])


def after(value, *others):
    return lax.optimization_barrier((value, others))[0]


def tile_of(rows, most=512):
    return most if rows % most == 0 else rows


def places_kernel(half, experts, where_ref, ids_ref, ranks_ref, keep_ref, gate_ref, out_ref, back_ref):
    me, core = where_ref[0], where_ref[1]
    ids, ranks, kept = ids_ref[...] ^ me, ranks_ref[...], keep_ref[...] == 1
    own = ranks - core * half
    out_ref[...] = jnp.where(kept & (own >= 0) & (own < half), ids * half + own, -1)
    upper = jnp.where(ranks >= half, 1, 0)
    back = ((upper ^ core) * experts + ids) * half + ranks - upper * half
    table = [jnp.where(kept, back, -1).astype(f32), gate_ref[...]]
    filler = jnp.zeros((8 - 2 * ids.shape[0], ids.shape[1]), f32)
    back_ref[...] = jnp.concatenate(table + [filler], 0).T


def slot_places(where, ids, ranks, keep, gates, half, experts):
    choices, rows = ids.shape
    return call(
        functools.partial(places_kernel, half, experts),
        [
            jax.ShapeDtypeStruct((choices, rows), jnp.int32),
            jax.ShapeDtypeStruct((rows, 8), f32),
        ],
        [SMEM] + [VMEM] * 4,
        [VMEM] * 2,
        [],
        8,
        rows * 64,
        rows * 512,
        where,
        ids,
        ranks,
        keep,
        gates,
    )


def dispatch_kernel(blocks, patches, per, where_ref, taps_ref, place_ref, *refs):
    tokens, refs = refs[:blocks], refs[blocks:]
    base_ref, outs, (extended, mixed_ref, sems) = refs[0], refs[1:-3], refs[-3:]
    rows = tokens[0].shape[0]
    copies = [
        pltpu.make_async_copy(
            tokens[i],
            extended.at[pl.ds(pl.multiple_of(where_ref[i] * rows, rows), rows)],
            sems.at[i],
        )
        for i in range(blocks)
    ]
    for copy in copies:
        copy.start()
    for copy in copies:
        copy.wait()
    frames = blocks * rows // patches
    width = extended.shape[1]
    for left in range(0, width, 128):
        lanes = slice(left, min(left + 128, width))
        taps = [taps_ref[i : i + 1, lanes] for i in range(3)]

        def step(t, carry, lanes=lanes, taps=taps):
            earlier, before = carry
            start = pl.multiple_of(t * patches, patches)
            now = extended[pl.ds(start, patches), lanes].astype(f32)
            mixed = taps[0] * now + taps[1] * before + taps[2] * earlier
            mixed_ref[pl.ds(start, patches), lanes] = mixed.astype(bf16)
            return before, now

        first = extended[0:patches, lanes].astype(f32)
        second = extended[patches : 2 * patches, lanes].astype(f32)
        mixed_ref[0:patches, lanes] = (taps[0] * first).astype(bf16)
        mixed_ref[patches : 2 * patches, lanes] = (taps[0] * second + taps[1] * first).astype(bf16)
        lax.fori_loop(2, frames, step, (first, second), unroll=3)

    place = place_ref[...]
    together = max(1, 512 // per)
    for base in range(0, len(outs), together):
        group = outs[base : base + together]
        size = per * len(group)
        slots = lax.broadcasted_iota(jnp.int32, (size, blocks * rows), 0) + base * per
        hit = (slots == place[0:1]) | (slots == place[1:2])
        picked = jnp.dot(
            jnp.where(hit, 1.0, 0.0).astype(bf16), mixed_ref[...], preferred_element_type=f32
        ).astype(bf16)
        for i, out in enumerate(group):
            out[...] = picked[i * per : (i + 1) * per]
    for i in range(blocks // 2):
        start = pl.multiple_of(where_ref[blocks + i] * rows, rows)
        base_ref[i * rows : (i + 1) * rows] = mixed_ref[pl.ds(start, rows)]


def mix_and_dispatch(where, taps, place, tokens, patches, experts, per):
    blocks = len(tokens)
    rows, cols = tokens[0].shape
    total = blocks * rows
    return call(
        functools.partial(dispatch_kernel, blocks, patches, per),
        [jax.ShapeDtypeStruct((total // 2, cols), bf16)]
        + [jax.ShapeDtypeStruct((per, cols), bf16)] * experts,
        [SMEM, VMEM, VMEM] + [HBM] * blocks,
        [VMEM] * (1 + experts),
        [
            pltpu.VMEM((total, cols), bf16),
            pltpu.VMEM((total, cols), bf16),
            pltpu.SemaphoreType.DMA((blocks,)),
        ],
        24,
        2 * total * per * experts * cols,
        total * cols * 2 + experts * per * cols * 2,
        where,
        taps,
        place,
        *tokens,
    )


def normalise(parts, starts, gain_ref, out):
    cols = parts[0].shape[1]
    scale = 1.0 / gain_ref.shape[1]
    values = [part.astype(f32) for part in parts]
    mean = sum(jnp.sum(value, -1, keepdims=True) for value in values) * scale
    values = [value - mean for value in values]
    spread = sum(jnp.sum(value * value, -1, keepdims=True) for value in values) * scale
    factor = lax.rsqrt(spread + eps)
    for value, start in zip(values, starts):
        at = pl.ds(start, cols)
        out[:, at] = (value * factor * gain_ref[:, at]).astype(bf16)


def in_place(chip, shares, cols, run):
    if cols % 128 == 0:
        run([pl.multiple_of((chip ^ d) * cols, 128) for d in range(shares)])
        return
    for i in range(shares):

        @pl.when(chip == i)
        def _(i=i):
            run([(i ^ d) * cols for d in range(shares)])


def expert_kernel(shares, where_ref, gain_ref, *refs):
    parts, refs = refs[:shares], refs[shares:]
    weights, refs = refs[:4], refs[4:]
    outs, refs = refs[:shares], refs[shares:]
    normed, hidden, held, sems = refs[0], refs[1], refs[2:6], refs[6]
    rows, cols = parts[0].shape
    copies = [
        pltpu.make_async_copy(weight, place, sems.at[i])
        for i, (weight, place) in enumerate(zip(weights, held))
    ]
    ups, downs = held[:2], held[2:]
    wide = ups[0].shape[1]
    step = 256 if wide % 256 == 0 else wide
    for copy in copies:
        copy.start()

    def run(starts):
        normalise([part[...] for part in parts], starts, gain_ref, normed)
        for i, up in enumerate(ups):
            copies[i].wait()
            for left in range(0, wide, step):
                product = jnp.dot(
                    normed[...], up[:, left : left + step], preferred_element_type=f32
                )
                at = i * wide + left
                hidden[:, at : at + step] = jax.nn.gelu(product).astype(bf16)
        copies[2].wait()
        copies[3].wait()
        for out, start in zip(outs, starts):
            at = pl.ds(start, cols)
            total = jnp.dot(hidden[:, :wide], downs[0][:, at], preferred_element_type=f32)
            total += jnp.dot(hidden[:, wide:], downs[1][:, at], preferred_element_type=f32)
            out[...] = total.astype(bf16)

    in_place(where_ref[0], shares, cols, run)


def expert_project(where, gain, parts, weights):
    rows, cols = parts[0].shape
    shares = len(parts)
    width, wide = weights[0].shape
    return call(
        functools.partial(expert_kernel, shares),
        [jax.ShapeDtypeStruct((rows, cols), bf16)] * shares,
        [SMEM, VMEM] + [VMEM] * shares + [HBM] * 4,
        [VMEM] * shares,
        [
            pltpu.VMEM((rows, width), bf16),
            pltpu.VMEM((rows, 2 * wide), bf16),
            pltpu.VMEM((width, wide), bf16),
            pltpu.VMEM((width, wide), bf16),
            pltpu.VMEM((wide, width), bf16),
            pltpu.VMEM((wide, width), bf16),
            pltpu.SemaphoreType.DMA((4,)),
        ],
        24,
        8 * rows * width * wide,
        8 * width * wide + rows * width * 4,
        where,
        gain,
        *parts,
        *weights,
    )


def sum_kernel(pieces, *refs):
    values, outs = refs[:pieces], refs[pieces:]
    rows = outs[0].shape[0]
    for i, out in enumerate(outs):
        at = slice(i * rows, (i + 1) * rows)
        total = values[0][at].astype(f32)
        for value in values[1:]:
            total = total + value[at].astype(f32)
        out[...] = total.astype(bf16)


def sum_blocks(values, blocks):
    rows, cols = values[0].shape
    return call(
        functools.partial(sum_kernel, len(values)),
        [jax.ShapeDtypeStruct((rows // blocks, cols), bf16)] * blocks,
        [VMEM] * len(values),
        [VMEM] * blocks,
        [],
        8,
        rows * cols * 2,
        rows * cols * 2 * (len(values) + 1),
        *values,
    )


def combine_kernel(firsts, skipped, where_ref, place_ref, base_ref, *refs):
    sources, out = refs[: len(firsts)], refs[len(firsts)]
    choices = 2
    rows = out.shape[0]
    start = pl.multiple_of(where_ref[0] * rows, rows)
    table = place_ref[pl.ds(start, rows)]
    place, gate = table[:, :choices].astype(jnp.int32), table[:, choices : 2 * choices]
    total = base_ref[skipped : skipped + rows].astype(f32)
    for first, source in zip(firsts, sources):
        many = source.shape[0]
        lanes = lax.broadcasted_iota(jnp.int32, (rows, many), 1) + first
        weight = jnp.zeros((rows, many), f32)
        for k in range(choices):
            weight = jnp.where(lanes == place[:, k : k + 1], gate[:, k : k + 1], weight)
        total = total + jnp.dot(weight.astype(bf16), source[...], preferred_element_type=f32)
    out[...] = total.astype(out.dtype)


def combine(where, places, base, sources, firsts, rows, skipped, dtype):
    cols = base.shape[1]
    many = sum(source.shape[0] for source in sources)
    return call(
        functools.partial(combine_kernel, firsts, skipped),
        jax.ShapeDtypeStruct((rows, cols), dtype),
        [SMEM, VMEM, VMEM] + [VMEM] * len(sources),
        VMEM,
        [],
        20,
        2 * rows * many * cols,
        rows * cols * 6 + many * cols * 2,
        where,
        places,
        base,
        *sources,
    )


def qkv_kernel(shares, block, quick, earlier, where_ref, gain_ref, weight_ref, *refs):
    parts, refs = refs[:shares], refs[shares + earlier :]
    out, refs = refs[0], refs[1:]
    if block is not None:
        stream, stage, stage_sem, refs = refs[0], refs[-2], refs[-1], refs[1:-2]
    normed, held, weights, sem, weight_sem = refs
    rows, cols = parts[0].shape
    heads = out.shape[1]
    loads = []
    for j in range(3):
        at = slice(j * heads, (j + 1) * heads)
        loads.append(
            pltpu.make_async_copy(weight_ref.at[at], weights.at[at], weight_sem.at[j])
        )
        loads[-1].start()

    to = pl.ds(pl.multiple_of(where_ref[1] * rows, rows), rows)
    copies = [
        pltpu.make_async_copy(
            held.at[j * heads : (j + 1) * heads], out.at[j, :, to], sem.at[j]
        )
        for j in range(3)
    ]
    tile = tile_of(rows, 256)

    def run(starts):
        if block is not None:
            @pl.when(where_ref[0] == block)
            def _():
                for part, start in zip(parts, starts):
                    stage[:, pl.ds(start, cols)] = part[...]
                pltpu.make_async_copy(stage, stream, stage_sem).start()

        def norm(at):
            normalise([part[at] for part in parts], starts, gain_ref, normed.at[at])

        def project(at):
            result = lax.dot_general(
                weights[...], normed[at], (((1,), (1,)), ((), ())), preferred_element_type=f32
            )
            held[:, at] = result.astype(bf16)

        def step(t, carry):
            at = pl.ds(pl.multiple_of(t * tile, tile), tile)
            norm(at)
            project(at)
            return carry

        tiles = [slice(left, left + tile) for left in range(0, rows, tile)]
        if quick:
            for at in tiles:
                norm(at)
        for load in loads:
            load.wait()
        if quick:
            for at in tiles:
                project(at)
        else:
            lax.fori_loop(0, rows // tile, step, 0)
        for copy in copies:
            copy.start()

    in_place(where_ref[0], shares, cols, run)
    for copy in copies:
        copy.wait()
    if block is not None:

        @pl.when(where_ref[0] == block)
        def _():
            pltpu.make_async_copy(stage, stream, stage_sem).wait()


def qkv_project(where, gain, weight, parts, total, block, quick, earlier):
    shares = len(parts)
    rows = parts[0].shape[0]
    wide, width = weight.shape
    shapes = [jax.ShapeDtypeStruct((3, wide // 3, total), bf16)]
    scratch = [
        pltpu.VMEM((rows, width), bf16),
        pltpu.VMEM((wide, rows), bf16),
        pltpu.VMEM((wide, width), bf16),
        pltpu.SemaphoreType.DMA((3,)),
        pltpu.SemaphoreType.DMA((3,)),
    ]
    if block is not None:
        shapes += [jax.ShapeDtypeStruct((rows, width), bf16)]
        scratch += [pltpu.VMEM((rows, width), bf16), pltpu.SemaphoreType.DMA]
    return pl.pallas_call(
        functools.partial(qkv_kernel, shares, block, quick, len(earlier)),
        out_shape=shapes,
        in_specs=[SMEM, VMEM, pl.BlockSpec(memory_space=pltpu.HBM)]
        + [VMEM] * shares
        + [HBM] * len(earlier),
        out_specs=[HBM] * len(shapes),
        scratch_shapes=scratch,
        input_output_aliases={3 + shares + i: i for i in range(len(earlier))},
        compiler_params=pltpu.CompilerParams(vmem_limit_bytes=20 << 20),
        cost_estimate=pl.CostEstimate(
            flops=2 * rows * width * wide,
            bytes_accessed=rows * (width + wide) * 2 + width * wide * 2,
            transcendentals=0,
        ),
    )(where, gain, weight, *parts, *earlier)


def local(
    tokens,
    time_taps,
    norm_gain,
    expert_ids,
    priority_ranks,
    keep_mask,
    gate_weights,
    up_weight,
    down_weight,
    attn_gain,
    qkv_weight,
):
    frames_here, patches, width = tokens.shape[1:]
    members = lax.axis_size("tm")
    experts = lax.axis_size("expert")
    chips = members // 2
    cols = width // chips
    place = lax.axis_index("tm")
    chip, core = place // 2, place % 2
    me = lax.axis_index("expert")
    own_rows = frames_here * patches
    rows = own_rows * members
    capacity = rows * expert_ids.shape[2] // (2 * experts)
    half = capacity // 2

    def columns_of(value, d):
        return lax.dynamic_slice_in_dim(value, (chip ^ d) * cols, cols, value.ndim - 1)

    def rows_of(value, i):
        return lax.dynamic_slice_in_dim(value, (2 * i + core) * own_rows, own_rows, 1)

    own_tokens = tokens.reshape(own_rows, width)
    theirs = [columns_of(own_tokens, d) for d in range(1, chips)]
    mine = columns_of(after(own_tokens, *theirs), 0)
    near = [mine] + [swap(value, "tm", 2 * d) for d, value in enumerate(theirs, 1)]
    over = [swap(value, "tm", 1) for value in near]
    token_places = jnp.stack(
        [(chip ^ d) * 2 + core for d in range(chips)]
        + [(chip ^ d) * 2 + 1 - core for d in range(chips)]
    ).astype(jnp.int32)

    ups = [up_weight[0], swap(up_weight[0], "tm", 1)]
    downs = [down_weight[0], swap(down_weight[0], "tm", 1)]
    qkv_columns = pltpu.with_memory_space_constraint(
        jnp.swapaxes(qkv_weight, 1, 2).reshape(-1, width), pltpu.HBM
    )
    taps = columns_of(time_taps, 0)

    where_chip = chip.astype(jnp.int32)[None]
    blocks_here = jnp.stack([2 * i + core for i in range(chips)]).astype(jnp.int32)
    out_place, back_place = slot_places(
        jnp.stack([me, core]).astype(jnp.int32),
        expert_ids[0].T,
        priority_ranks[0].T,
        keep_mask[0].T,
        gate_weights[0].T,
        half,
        experts,
    )

    weights = ups + downs
    near, over, weights, out_place = lax.optimization_barrier((near, over, weights, out_place))
    base, *sent = mix_and_dispatch(
        jnp.concatenate([token_places, blocks_here]),
        taps,
        out_place,
        near + over,
        patches,
        experts,
        half,
    )

    middle = experts // 2
    bounds = [0, middle // 2, middle, middle + middle // 2, experts]
    groups = [range(*pair) for pair in zip(bounds, bounds[1:])]
    arrived = [sent[0]] + [swap(sent[k], "expert", k) for k in range(1, groups[2].stop)]
    partial_sums = []
    for group in groups:
        rows_in = jnp.concatenate([arrived[k] for k in group], 0)
        shares = [rows_in] + [swap(rows_in, "tm", 2 * d) for d in range(1, chips)]
        if not partial_sums:
            last = after([sent[k] for k in groups[3]], *shares[1:])
            arrived += [swap(value, "expert", k) for k, value in zip(groups[3], last)]
        else:
            shares = after(shares, *partial_sums[-1])
        partial_sums.append(expert_project(where_chip, norm_gain[None], shares, weights))

    returned = [None] * len(groups)
    received = [None] * len(groups)
    sent_back = [None] * len(groups)
    for g, follows in ((2, None), (3, None), (1, 2), (0, 3)):
        sums = list(partial_sums[g])
        if follows:
            sums = after(sums, *sent_back[follows])
        received[g] = [swap(sums[d], "tm", 2 * d) for d in range(1, chips)]
        sent_back[g] = sum_blocks([sums[0]] + received[g], len(groups[g]))
        returned[g] = [
            swap(block, "expert", k) if k else block for k, block in zip(groups[g], sent_back[g])
        ]
    returned = after(returned, *received[0], *received[1])
    back = [jnp.concatenate(blocks, 0) for blocks in returned]
    over_back = [swap(value, "tm", 1) for value in back]
    tables = [(g, side) for side in range(2) for g in range(len(groups))]
    first_steps = [[(2, 0), (2, 1)], [(0, 0), (1, 0), (3, 0)], [(0, 1), (1, 1), (3, 1)]]
    stream = []
    for i in range(chips):
        total, skipped = base, i * own_rows
        steps = [tables] if i else first_steps
        for step in steps:
            sources = [(over_back if side else back)[g] for g, side in step]
            firsts = [(side * experts + groups[g].start) * half for g, side in step]
            total = combine(
                blocks_here[i : i + 1],
                back_place,
                total,
                sources,
                firsts,
                own_rows,
                skipped,
                bf16 if step is steps[-1] else f32,
            )
            skipped = 0
        stream.append(total)

    qkv_rows, own_stream, before = [], [], None
    for i in range(chips):
        if before:
            stream[i] = after(stream[i], *before)
        pieces = [stream[i]] + [swap(stream[i], "tm", 2 * d) for d in range(1, chips)]
        before = pieces
        if i < chips - 1:
            pieces = after(pieces, stream[i + 1])
        if i:
            pieces = after(pieces, *qkv_rows)
        other = [swap(piece, "tm", 1) for piece in pieces]
        for side, parts in ((core, pieces), (1 - core, other)):
            own = parts is pieces
            done = qkv_project(
                jnp.stack([chip, 2 * i + side]).astype(jnp.int32),
                attn_gain[None],
                qkv_columns,
                parts,
                rows,
                i if own else None,
                i == chips - 1,
                qkv_rows + (own_stream if own else []),
            )
            qkv_rows, own_stream = [done[0]], [done[1]] if own else own_stream
    return (own_stream[0].reshape(tokens.shape), jnp.swapaxes(qkv_rows[0], 1, 2)[:, None])


def solution(mesh):
    in_specs = (
        P("expert", "tm", None, None),
        P(),
        P(),
        P("expert", None, None),
        P("expert", None, None),
        P("expert", None, None),
        P("expert", None, None),
        P("expert", None, "tm"),
        P("expert", "tm", None),
        P(),
        P(None, None, "tm"),
    )
    out_specs = (P("expert", "tm", None, None), P(None, "expert", None, "tm"))
    return jax.shard_map(local, mesh=mesh, in_specs=in_specs, out_specs=out_specs, check_vma=False)
```
